32 devices in a mesh: patch: 8 (over y, x, core), head: 4 (over z).
Axes of the slice: x: 2, y: 2, z: 4, core: 2. Of those that a mesh axis runs over, the one named last changes fastest.
Arguments:
- fresh_qkv: bfloat16 [4096, 3, 3072], P('patch', None, 'head'), may hold values from -12 to 12
- kv_cache: bfloat16 [4096, 2, 3072], P('patch', None, 'head'), may hold values from -8 to 8
- hidden: bfloat16 [4096, 3072], P('patch'), may hold values from -6 to 6
- refresh: int32 [4], replicated, may hold values from 0 to 7, as said below
- out_weight: bfloat16 [3072, 3072], P('head'), may hold values from -0.109375 to 0.109375
- final_weight: bfloat16 [3072, 64], replicated, may hold values from -0.109375 to 0.109375
- final_bias: float32 [64], replicated, may hold values from -3 to 3
- gate_scale: float32 [3072], replicated, may hold values from 0.1 to 1.9
- noise_level: float32 [1], replicated, may hold values from 0.15 to 0.35
- noisy_latent: bfloat16 [16, 16, 1024], P('patch'), may hold values from -6 to 6
- velocity_cache: bfloat16 [16, 16, 1024], P('patch'), may hold values from -6 to 6
- conv_weight: bfloat16 [512, 3, 3, 16], P('head'), may hold values from -0.5 to 0.5
- conv_bias: float32 [512], P('head'), may hold values from -3 to 3
Outputs:
- decoded: bfloat16 [16, 512, 1024], P('patch', 'head')
The draws below stay inside these ranges and needn't reach their ends.
Inputs may be any that keep to these rules, and one draw needn't show every extreme that they name: 4 distinct patch indices; refresh[1] is 7.
All inputs are finite; a program needn't handle non-finite values.
Results may differ from the reference program's by a relative error of at most 0.0044.
The reference program's roundings to bfloat16 on the way count: a program that leaves them out, or rounds other values in their place, can miss the bound.
Values may be sent and summed in bfloat16 or wider, within the bound.
A program may use at most 128 MiB of HBM per device.

```python
import math
import jax
import jax.numpy as jnp
from jax import lax

D = 3072
HEADS = 24
HEAD_DIM = 128
LAT_CH = 16
CONV_CH = 512
GW = 512
ROWS_DEV = 1
REFRESH = 4
PATCH_VEC = 64
TOK_DEV = 512
PATCHES = 8
TOKENS = 4096
NQ = 2048
LROWS = 16
LW = 1024


def draw_fresh_qkv(key, part):
    first_key = jax.random.fold_in(key, 0)
    background = jnp.clip(2.0 * jax.random.normal(first_key, (TOKENS, 3, D), jnp.float32), -8.0, 8.0)
    return background.astype(jnp.bfloat16)


def draw_refresh(key, part):
    others = jax.random.permutation(key, PATCHES - 1)[:REFRESH - 1].astype(jnp.int32)
    last_patch = jnp.full((1,), PATCHES - 1, dtype=jnp.int32)
    return jnp.concatenate([others[:1], last_patch, others[1:]], axis=0)


def levels(rng, shape, cuts, low, high):
    def one(dim, shards_of):
        heights = jax.random.uniform(jax.random.fold_in(jax.random.fold_in(rng, 6), dim), (shards_of,), jnp.float32, low / len(cuts), high / len(cuts))
        return jnp.repeat(jnp.exp(heights), shape[dim] // shards_of).reshape((-1,) + (1,) * (len(shape) - dim - 1))

    gain = one(*cuts[0])
    for cut in cuts[1:]:
        gain = gain * one(*cut)
    return gain


def bell_draw(stream_key, dims, scale, limit, shards=(), held_as=jnp.bfloat16):
    gain = levels(stream_key, dims, shards, -0.22, 0.18) if shards else 1.0
    result = jax.random.normal(stream_key, dims, jnp.float32) * scale * gain
    return jnp.minimum(jnp.maximum(result, -limit), limit).astype(held_as)


def setup_inputs(seed: int = 0) -> dict:
    key_list = jax.random.split(jax.random.key(seed), 14)
    fresh_qkv = draw_fresh_qkv(jax.random.fold_in(key_list[13], 71), 0)
    kv_cache = bell_draw(key_list[1], (TOKENS, 2, D), 2.0, 8.0, ((0, 8), (2, 4)))
    hidden = bell_draw(key_list[2], (TOKENS, D), 1.0, 6.0, ((0, 8),))
    refresh = draw_refresh(jax.random.fold_in(key_list[13], 71), 0)
    out_weight = bell_draw(key_list[4], (D, D), D ** -0.5, 0.109375, ((0, 4),))
    final_weight = bell_draw(key_list[5], (D, PATCH_VEC), D ** -0.5, 0.109375)
    final_bias = bell_draw(key_list[6], (PATCH_VEC,), 0.5, 3.0, (), jnp.float32)
    gate_scale = jnp.clip(1.0 + 0.18 * jax.random.normal(key_list[7], (D,), jnp.float32), 0.1, 1.9)
    noise_level = jnp.clip(jax.random.uniform(key_list[8], (1,), jnp.float32, 0.15, 0.35), 0.15, 0.35)
    noisy_latent = bell_draw(key_list[9], (LROWS, LAT_CH, LW), 1.0, 6.0, ((0, 8),))
    velocity_cache = bell_draw(key_list[10], (LROWS, LAT_CH, LW), 1.0, 6.0, ((0, 8),))
    conv_weight = bell_draw(key_list[11], (CONV_CH, 3, 3, LAT_CH), (9 * LAT_CH) ** -0.5, 0.5, ((0, 4),))
    conv_bias = bell_draw(key_list[12], (CONV_CH,), 0.5, 3.0, ((0, 4),), jnp.float32)
    return dict(fresh_qkv=fresh_qkv, kv_cache=kv_cache, hidden=hidden, refresh=refresh, out_weight=out_weight, final_weight=final_weight, final_bias=final_bias, gate_scale=gate_scale, noise_level=noise_level, noisy_latent=noisy_latent, velocity_cache=velocity_cache, conv_weight=conv_weight, conv_bias=conv_bias)


def reference(fresh_qkv, kv_cache, hidden, refresh, out_weight, final_weight, final_bias, gate_scale, noise_level, noisy_latent, velocity_cache, conv_weight, conv_bias):
    patch_ids = jnp.arange(PATCHES, dtype=jnp.int32)
    chosen = jnp.any(patch_ids[:, None] == refresh[None, :], axis=1)
    token_chosen = jnp.repeat(chosen, TOK_DEV)
    key_rows = jnp.where(token_chosen[:, None], fresh_qkv[:, 1], kv_cache[:, 0])
    value_rows = jnp.where(token_chosen[:, None], fresh_qkv[:, 2], kv_cache[:, 1])
    queries = fresh_qkv.reshape(PATCHES, TOK_DEV, 3, D)[refresh][:, :, 0].reshape(NQ, D)
    block_rows = math.gcd(NQ, 512)
    score_scale = 1.0 / math.sqrt(HEAD_DIM)

    def one_head(head_number):
        head_start = (head_number * HEAD_DIM).astype(jnp.int32)
        head_queries = lax.dynamic_slice_in_dim(queries, head_start, HEAD_DIM, 1)
        head_keys = lax.dynamic_slice_in_dim(key_rows, head_start, HEAD_DIM, 1)
        head_values = lax.dynamic_slice_in_dim(value_rows, head_start, HEAD_DIM, 1)

        def one_block(block_number):
            row_start = (block_number * block_rows).astype(jnp.int32)
            row_block = lax.dynamic_slice_in_dim(head_queries, row_start, block_rows, 0)
            scores = jnp.dot(row_block, head_keys.T, preferred_element_type=jnp.float32) * score_scale
            row_max = lax.optimization_barrier(jnp.max(scores, axis=1, keepdims=True))
            exp_scores = jnp.exp(scores - row_max)
            denominator = lax.optimization_barrier(jnp.sum(exp_scores, axis=1, keepdims=True))
            numerator = jnp.dot(exp_scores.astype(jnp.bfloat16), head_values, preferred_element_type=jnp.float32)
            return numerator / denominator
        return lax.map(one_block, jnp.arange(NQ // block_rows, dtype=jnp.int32)).reshape(NQ, HEAD_DIM)
    attention = lax.map(one_head, jnp.arange(HEADS, dtype=jnp.int32))
    attention = jnp.transpose(attention, (1, 0, 2)).reshape(NQ, D)
    projected = jnp.dot(attention, out_weight.astype(jnp.float32), precision=lax.Precision.HIGHEST)
    hidden_rows = hidden.reshape(PATCHES, TOK_DEV, D)[refresh].reshape(NQ, D)
    velocity_fresh = jnp.dot(hidden_rows, final_weight, preferred_element_type=jnp.float32) + final_bias
    velocity_fresh = velocity_fresh + jnp.dot(gate_scale[None, :] * projected, final_weight.astype(jnp.float32), precision=lax.Precision.HIGHEST)
    fresh_field = velocity_fresh.reshape(REFRESH, ROWS_DEV, GW, LAT_CH, 2, 2)
    fresh_field = jnp.transpose(fresh_field, (0, 1, 4, 3, 2, 5)).reshape(REFRESH, 2 * ROWS_DEV, LAT_CH, LW)
    velocity_field = velocity_cache.astype(jnp.float32).reshape(PATCHES, 2 * ROWS_DEV, LAT_CH, LW)
    velocity_field = velocity_field.at[refresh].set(fresh_field).reshape(LROWS, LAT_CH, LW)
    latent = noisy_latent.astype(jnp.float32) - noise_level[0] * velocity_field
    decoder_in = (latent / 0.3611 + 0.1159).astype(jnp.bfloat16)
    padded = jnp.pad(decoder_in, ((1, 1), (0, 0), (1, 1)))
    stencil = jnp.stack([padded[row_shift:row_shift + LROWS, :, col_shift:col_shift + LW] for row_shift in range(3) for col_shift in range(3)], axis=1)
    stencil = stencil.reshape(LROWS, 9 * LAT_CH, LW)
    kernel = conv_weight.reshape(CONV_CH, 9 * LAT_CH)
    decoded = jnp.einsum('oc,rcw->row', kernel.astype(jnp.float32), stencil.astype(jnp.float32))
    decoded = decoded + conv_bias[None, :, None]
    return decoded.astype(jnp.bfloat16)
```

```python
import functools
import math

import jax
import jax.numpy as jnp
from jax import lax
from jax.experimental import pallas as pl
from jax.experimental.pallas import tpu as pltpu
from jax.sharding import PartitionSpec as P

HEAD_DIM = 128
LAT_CH = 16
REFRESH = 4
MESH = pl.DeviceIdType.MESH
SCALE2 = math.log2(math.e) / math.sqrt(HEAD_DIM)
NT = (((1,), (1,)), ((), ()))
TN = (((0,), (0,)), ((), ()))
F32 = jnp.float32
BF16 = jnp.bfloat16


def iota(shape, dim):
    return lax.broadcasted_iota(jnp.int32, shape, dim)


def q_slots(n, heads):
    return heads if n == 8 else min(2, heads)


def to_column(row):
    size = row.shape[1]
    eye = iota((size, size), 0) == iota((size, size), 1)
    return jnp.sum(jnp.where(eye, row, 0.0), axis=1, keepdims=True)


def kernel(
    n,
    nz,
    heads,
    tok,
    refresh,
    noise,
    fresh,
    kv,
    hidden,
    out_weight,
    final_t,
    bias,
    gate,
    noisy,
    cache,
    conv_t,
    conv_bias,
    out,
    *scratch,
):
    slots = q_slots(n, heads)
    q_all = [scratch[h % slots] for h in range(heads)]
    stats = scratch[slots : slots + heads]
    (
        fresh_kv,
        hidden_v,
        weight_v,
        keys,
        values_t,
        w2,
        u_buf,
        spread,
        hid_t,
        rs_out,
        rs_in,
        z_buf,
        ag,
        dec,
        halo,
        load_sem,
        own_sem,
        q_send,
        q_recv,
        st_send,
        st_recv,
        rs_send,
        rs_recv,
        z_send,
        z_recv,
        ag_send,
        ag_recv,
        halo_send,
        halo_recv,
        free_sem,
    ) = scratch[slots + heads :]
    me = lax.axis_index("patch")
    mz = lax.axis_index("head")
    vec = final_t.shape[0]
    rows = vec // n

    def peers(count, body):
        if count <= 8:
            for step in range(1, count):
                body(step)
        else:
            pl.loop(1, count)(body)

    def other(step):
        return lax.rem(me + step, n)

    def other_z(step):
        return lax.rem(mz + step, nz)

    def remote(src, dst, send, recv, **where):
        return pltpu.make_async_remote_copy(
            src_ref=src,
            dst_ref=dst,
            send_sem=send,
            recv_sem=recv,
            device_id=where,
            device_id_type=MESH,
        )

    loads = [
        pltpu.make_async_copy(fresh.at[1], fresh_kv.at[0], load_sem.at[0]),
        pltpu.make_async_copy(fresh.at[2], fresh_kv.at[1], load_sem.at[1]),
        pltpu.make_async_copy(out_weight, weight_v, load_sem.at[2]),
        pltpu.make_async_copy(hidden, hidden_v, load_sem.at[3]),
    ]
    own_q = [fresh.at[0, :, pl.ds(h * HEAD_DIM, HEAD_DIM)] for h in range(heads)]
    own_copies = [
        pltpu.make_async_copy(own_q[h], q_all[h].at[me], own_sem.at[h]) for h in range(heads)
    ]
    for copy in loads + own_copies[:slots]:
        copy.start()

    barrier = pltpu.get_barrier_semaphore()
    peers(n, lambda d: pl.semaphore_signal(
        barrier, inc=1, device_id={"patch": other(d)}, device_id_type=MESH))
    peers(nz, lambda d: pl.semaphore_signal(
        barrier, inc=1, device_id={"head": other_z(d)}, device_id_type=MESH))
    pl.semaphore_wait(barrier, n - 1 + nz - 1)

    if n == 8:
        near = me + 1 - 2 * lax.rem(me, 2)
        side = me + 2 - 4 * lax.rem(me // 2, 2)
        over = me + 4 - 8 * (me // 4)
        diag = side + over - me
        half = tok // 2
        low, high = pl.ds(0, half), pl.ds(half, half)
        near_of = lambda p: p + near - me

        def q_copy(h, kind, src, dst, to):
            return remote(src, dst, q_send.at[h, kind], q_recv.at[h, kind], patch=to)

        def first(h):
            dst = q_all[h].at[me]
            return [q_copy(h, k, own_q[h], dst, to) for k, to in ((0, side), (1, over), (2, near))]

        def second(h):
            from_side, from_over = q_all[h].at[side], q_all[h].at[over]
            return [
                q_copy(h, 3, from_side.at[low], from_side.at[low], over),
                q_copy(h, 4, from_over.at[high], from_over.at[high], side),
                q_copy(h, 5, from_side, from_side, near),
                q_copy(h, 6, from_over, from_over, near),
            ]

        def third(h):
            block = q_all[h].at[diag]
            return [q_copy(h, 7, block, block, near)]

        def arrive(h, kind, dst):
            q_copy(h, kind, dst, dst, near).wait_recv()

        def start(copies):
            for copy in copies:
                copy.start()

        def relay(h):
            arrive(h, 0, q_all[h].at[side])
            arrive(h, 1, q_all[h].at[over])
            start(second(h))

        def relay_last(h):
            arrive(h, 3, q_all[h].at[diag].at[low])
            arrive(h, 4, q_all[h].at[diag].at[high])
            start(third(h))

        def before(h):
            if h + 2 < heads:
                start(first(h + 2))
            if h + 1 < heads:
                relay(h + 1)
            relay_last(h)
            arrive(h, 2, q_all[h].at[near])
            arrive(h, 5, q_all[h].at[near_of(side)])
            arrive(h, 6, q_all[h].at[near_of(over)])
            arrive(h, 7, q_all[h].at[near_of(diag)])

        def prologue():
            for h in range(min(2, heads)):
                start(first(h))

        def middle():
            relay(0)

        def refill(h):
            pass

        def sent():
            for h in range(heads):
                for copy in first(h) + second(h) + third(h):
                    copy.wait_send()

    else:

        def direct(h, d):
            return remote(
                own_q[h], q_all[h].at[me], q_send.at[h, d], q_recv.at[h, d], patch=other(d)
            )

        def prologue():
            for h in range(slots):
                peers(n, lambda d: direct(h, d).start())

        def refill(h):
            later = h + slots
            if later < heads:
                peers(n, lambda d: pl.semaphore_signal(
                    free_sem.at[h], inc=1, device_id={"patch": other(d)}, device_id_type=MESH))
                pl.semaphore_wait(free_sem.at[h], n - 1)
                own_copies[later].start()
                peers(n, lambda d: direct(later, d).start())

        def middle():
            pass

        def before(h):
            peers(n, lambda d: direct(h, d).wait_recv())

        def sent():
            for h in range(heads):
                peers(n, lambda d: direct(h, d).wait_send())

    prologue()

    is_mine = [refresh[s] == me for s in range(REFRESH)]
    mine = is_mine[0] | is_mine[1] | is_mine[2] | is_mine[3]
    group = 128
    r, c = iota((2 * group, 2 * group), 0), iota((2 * group, 2 * group), 1)
    unmix = (c == jnp.where(r < group, 2 * r, 2 * (r - group) + 1)).astype(BF16)
    eye = (iota((HEAD_DIM, HEAD_DIM), 0) == iota((HEAD_DIM, HEAD_DIM), 1)).astype(BF16)
    loads[0].wait()
    loads[1].wait()
    for g in range(tok // group):
        at = pl.ds(g * group, group)
        mixed = jnp.dot(unmix, kv[pl.ds(2 * g * group, 2 * group), :], preferred_element_type=F32)
        mixed = mixed.astype(BF16)
        keys[at, :] = jnp.where(mine, fresh_kv[0, at, :], mixed[:group])
        picked = jnp.where(mine, fresh_kv[1, at, :], mixed[group:])
        for h in range(heads):
            cols = slice(h * HEAD_DIM, (h + 1) * HEAD_DIM)
            values_t[h, :, at] = lax.dot_general(
                eye, picked[:, cols], NT, preferred_element_type=F32
            ).astype(BF16)
    middle()

    k_of = iota((vec, vec), 1)
    r_of = iota((vec, vec), 0)
    row_k = (r_of & (LAT_CH - 1)) * 4 + (r_of >> 5) * 2 + ((r_of >> 4) & 1)
    order = k_of == row_k
    final_rows = jnp.dot(order.astype(BF16), final_t[...], preferred_element_type=F32)
    gated = final_rows * gate[...]
    gated_hi = gated.astype(BF16)
    gated_lo = (gated - gated_hi.astype(F32)).astype(BF16)
    loads[2].wait()
    w2_f = lax.dot_general(
        jnp.concatenate([gated_hi, gated_lo], axis=0), weight_v[...], NT, preferred_element_type=F32
    )
    w2_f = w2_f[:vec] + w2_f[vec:]
    w2_hi = w2_f.astype(BF16)
    w2[:vec, :] = w2_hi
    w2[vec:, :] = (w2_f - w2_hi.astype(F32)).astype(BF16)
    loads[3].wait()
    bias_col = jnp.sum(jnp.where(order, bias[...], 0.0), axis=1, keepdims=True)
    hid_t[...] = bias_col + lax.dot_general(
        final_rows.astype(BF16), hidden_v[...], NT, preferred_element_type=F32
    )
    rr, cc = iota(spread.shape, 0), iota(spread.shape, 1)
    spread[...] = (cc == jnp.where(rr < tok, 2 * rr, 2 * (rr - tok) + 1)).astype(BF16)

    def st_copy(h, d):
        part = stats[h].at[me]
        return remote(part, part, st_send.at[h, d], st_recv.at[h, d], patch=other(d))

    for h in range(heads):
        own_copies[h].wait()
        before(h)
        cols = slice(h * HEAD_DIM, (h + 1) * HEAD_DIM)

        @pl.loop(0, REFRESH)
        def _(s):
            query = q_all[h][refresh[s]]
            scores = lax.dot_general(keys[:, cols], query, NT, preferred_element_type=F32)
            top = jnp.max(scores, axis=0, keepdims=True)
            weights = jnp.exp2((scores - top) * SCALE2)
            stats[h][me, pl.ds(s, 1), :] = top
            stats[h][me, pl.ds(s + REFRESH, 1), :] = jnp.sum(weights, axis=0, keepdims=True)
            num = jnp.dot(values_t[h], weights.astype(BF16), preferred_element_type=F32)
            num_hi = num.astype(BF16)
            num_lo = (num - num_hi.astype(F32)).astype(BF16)
            both = jnp.dot(w2[:, cols], num_hi, preferred_element_type=F32)
            rest = jnp.dot(w2[:vec, cols], num_lo, preferred_element_type=F32)
            u_buf[h, s] = both[:vec] + both[vec:] + rest

        peers(n, lambda d: st_copy(h, d).start())
        refill(h)

    sums = [jnp.zeros((vec, tok), F32) for _ in range(REFRESH)]
    for h in range(heads):
        peers(n, lambda d: st_copy(h, d).wait_recv())
        every = stats[h][...]
        tops, dens = every[:, :REFRESH], every[:, REFRESH:]
        top = jnp.max(tops, axis=0)
        den = jnp.sum(dens * jnp.exp2((tops - top[None]) * SCALE2), axis=0)
        factor = jnp.exp2((stats[h][me][:REFRESH] - top) * SCALE2) / den
        for s in range(REFRESH):
            sums[s] = sums[s] + u_buf[h, s] * factor[s : s + 1]
    for p in range(n):
        for s in range(REFRESH):
            rs_out[p, s] = sums[s][p * rows : (p + 1) * rows]

    def rs_copy(d):
        to = other(d)
        return remote(rs_out.at[to], rs_in.at[d], rs_send.at[d], rs_recv.at[d], patch=to)

    peers(n, lambda d: rs_copy(d).start())
    peers(n, lambda d: rs_copy(d).wait_recv())
    total = rs_out[me]
    for d in range(1, n):
        total = total + rs_in[d]
    z_buf[mz] = total

    def z_copy(d):
        part = z_buf.at[mz]
        return remote(part, part, z_send.at[d], z_recv.at[d], head=other_z(d))

    peers(nz, lambda d: z_copy(d).start())
    peers(nz, lambda d: z_copy(d).wait_recv())
    total = z_buf[0]
    for d in range(1, nz):
        total = total + z_buf[d]
    ag[me] = total

    def ag_copy(d):
        part = ag.at[me]
        return remote(part, part, ag_send.at[d], ag_recv.at[d], patch=other(d))

    peers(n, lambda d: ag_copy(d).start())
    peers(n, lambda d: ag_copy(d).wait_recv())
    parts = []
    for p in range(n):
        part = jnp.zeros((rows, tok), F32)
        for s in range(REFRESH):
            part = jnp.where(is_mine[s], ag[p, s], part)
        parts.append(part)
    velocity = jnp.concatenate(parts, axis=0) + hid_t[...]
    wide = [
        jnp.concatenate([velocity[a * 32 : a * 32 + 16], velocity[a * 32 + 16 : a * 32 + 32]], axis=1)
        for a in range(2)
    ]
    wide = jnp.concatenate(wide, axis=0)
    one = wide.astype(BF16)
    left = wide - one.astype(F32)
    two = left.astype(BF16)
    three = (left - two.astype(F32)).astype(BF16)
    pieces = jnp.dot(
        jnp.concatenate([one, two, three], axis=0), spread[...], preferred_element_type=F32
    )
    field = pieces[:32] + pieces[32:64] + pieces[64:]
    for a in range(2):
        fresh_row = field[a * LAT_CH : (a + 1) * LAT_CH]
        row = jnp.where(mine, fresh_row, cache[a].astype(F32))
        latent = noisy[a].astype(F32) - noise[0] * row
        dec[a] = (latent / 0.3611 + 0.1159).astype(BF16)

    after, prior = lax.rem(me + 1, n), lax.rem(me + n - 1, n)
    edges = [
        remote(dec.at[1], halo.at[0], halo_send.at[0], halo_recv.at[0], patch=after),
        remote(dec.at[0], halo.at[1], halo_send.at[1], halo_recv.at[1], patch=prior),
    ]
    for copy in edges:
        copy.start()
    for copy in edges:
        copy.wait_recv()
    lines = [
        jnp.where(me > 0, halo[0].astype(F32), 0.0),
        dec[0].astype(F32),
        dec[1].astype(F32),
        jnp.where(me < n - 1, halo[1].astype(F32), 0.0),
    ]
    width = dec.shape[2]
    column = iota((LAT_CH, width), 1)
    shifted = []
    for line in lines:
        before_it = jnp.where(column == 0, 0.0, pltpu.roll(line, 1, 1))
        after_it = jnp.where(column == width - 1, 0.0, pltpu.roll(line, width - 1, 1))
        shifted.append([x.astype(BF16) for x in (before_it, line, after_it)])
    conv_col = to_column(conv_bias[...])
    for a in range(2):
        stencil = jnp.concatenate([shifted[a + u][v] for u in range(3) for v in range(3)], axis=0)
        result = lax.dot_general(conv_t[...], stencil, TN, preferred_element_type=F32)
        out[a] = (result + conv_col).astype(BF16)

    sent()
    for h in range(heads):
        peers(n, lambda d: st_copy(h, d).wait_send())
    peers(n, lambda d: rs_copy(d).wait_send())
    peers(nz, lambda d: z_copy(d).wait_send())
    peers(n, lambda d: ag_copy(d).wait_send())
    for copy in edges:
        copy.wait_send()


def on_device(
    n,
    nz,
    fresh_qkv,
    kv_cache,
    hidden,
    refresh,
    out_weight,
    final_weight,
    final_bias,
    gate_scale,
    noise_level,
    noisy_latent,
    velocity_cache,
    conv_weight,
    conv_bias,
):
    tok, _, local = fresh_qkv.shape
    heads = local // HEAD_DIM
    depth, vec = final_weight.shape
    rows = vec // n
    width = noisy_latent.shape[2]
    channels = conv_weight.shape[0]
    vmem, smem, anyw = (pl.BlockSpec(memory_space=m) for m in (pltpu.VMEM, pltpu.SMEM, pl.ANY))
    dma = pltpu.SemaphoreType.DMA
    kinds = 8 if n == 8 else n
    scratch = (
        [pltpu.VMEM((n, tok, HEAD_DIM), BF16)] * q_slots(n, heads)
        + [pltpu.VMEM((n, 2 * REFRESH, tok), F32)] * heads
        + [
            pltpu.VMEM((2, tok, local), BF16),
            pltpu.VMEM((tok, depth), BF16),
            pltpu.VMEM((local, depth), BF16),
            pltpu.VMEM((tok, local), BF16),
            pltpu.VMEM((heads, HEAD_DIM, tok), BF16),
            pltpu.VMEM((2 * vec, local), BF16),
            pltpu.VMEM((heads, REFRESH, vec, tok), F32),
            pltpu.VMEM((2 * tok, 2 * tok), BF16),
            pltpu.VMEM((vec, tok), F32),
            pltpu.VMEM((n, REFRESH, rows, tok), F32),
            pltpu.VMEM((n, REFRESH, rows, tok), F32),
            pltpu.VMEM((nz, REFRESH, rows, tok), F32),
            pltpu.VMEM((n, REFRESH, rows, tok), F32),
            pltpu.VMEM((2, LAT_CH, width), BF16),
            pltpu.VMEM((2, LAT_CH, width), BF16),
            dma((4,)),
            dma((heads,)),
            dma((heads, kinds)),
            dma((heads, kinds)),
            dma((heads, n)),
            dma((heads, n)),
            dma((n,)),
            dma((n,)),
            dma((nz,)),
            dma((nz,)),
            dma((n,)),
            dma((n,)),
            dma((2,)),
            dma((2,)),
            pltpu.SemaphoreType.REGULAR((heads,)),
        ]
    )
    return pl.pallas_call(
        functools.partial(kernel, n, nz, heads, tok),
        out_shape=jax.ShapeDtypeStruct((2, channels, width), BF16),
        in_specs=[smem, smem, anyw, vmem, anyw, anyw] + [vmem] * 7,
        out_specs=vmem,
        scratch_shapes=scratch,
        compiler_params=pltpu.CompilerParams(
            collective_id=0, has_side_effects=True, vmem_limit_bytes=58 * 1024 * 1024
        ),
    )(
        refresh,
        noise_level,
        jnp.transpose(fresh_qkv, (1, 0, 2)),
        kv_cache.reshape(2 * tok, local),
        hidden,
        out_weight,
        final_weight.T,
        final_bias[None, :],
        gate_scale[None, :],
        noisy_latent,
        velocity_cache,
        jnp.transpose(conv_weight, (1, 2, 3, 0)).reshape(-1, channels),
        conv_bias[None, :],
    )


def solution(mesh):
    return jax.shard_map(
        functools.partial(on_device, mesh.shape["patch"], mesh.shape["head"]),
        mesh=mesh,
        in_specs=(
            P("patch", None, "head"),
            P("patch", None, "head"),
            P("patch", None),
            P(),
            P("head", None),
            P(),
            P(),
            P(),
            P(),
            P("patch", None, None),
            P("patch", None, None),
            P("head", None, None, None),
            P("head"),
        ),
        out_specs=P("patch", "head", None),
        check_vma=False,
    )
```

```python
import functools
import math

import jax
import jax.numpy as jnp
from jax import lax
from jax.experimental import pallas as pl
from jax.experimental.pallas import tpu as pltpu
from jax.sharding import PartitionSpec as P

HEAD_DIM = 128
LAT_CH = 16
REFRESH = 4
MESH = pl.DeviceIdType.MESH
SCALE2 = math.log2(math.e) / math.sqrt(HEAD_DIM)
NT = (((1,), (1,)), ((), ()))
TN = (((0,), (0,)), ((), ()))
F32 = jnp.float32
BF16 = jnp.bfloat16


def iota(shape, dim):
    return lax.broadcasted_iota(jnp.int32, shape, dim)


def q_slots(n, heads):
    return heads if n == 8 else min(2, heads)


def to_column(row):
    size = row.shape[1]
    eye = iota((size, size), 0) == iota((size, size), 1)
    return jnp.sum(jnp.where(eye, row, 0.0), axis=1, keepdims=True)


def kernel(
    n,
    nz,
    heads,
    tok,
    refresh,
    noise,
    fresh,
    kv,
    hidden,
    out_weight,
    final_t,
    bias,
    gate,
    noisy,
    cache,
    conv_t,
    conv_bias,
    out,
    *scratch,
):
    slots = q_slots(n, heads)
    q_all = [scratch[h % slots] for h in range(heads)]
    stats = scratch[slots : slots + heads]
    (
        fresh_kv,
        hidden_v,
        weight_v,
        keys,
        values_t,
        w2,
        u_buf,
        spread,
        hid_t,
        rs_out,
        rs_in,
        z_out,
        z_in,
        z_all,
        ag_out,
        ag,
        dec,
        halo,
        load_sem,
        own_sem,
        q_send,
        q_recv,
        st_send,
        st_recv,
        rs_send,
        rs_recv,
        z_send,
        z_recv,
        zg_send,
        zg_recv,
        ag_send,
        ag_recv,
        halo_send,
        halo_recv,
        free_sem,
    ) = scratch[slots + heads :]
    me = lax.axis_index("patch")
    mz = lax.axis_index("head")
    vec = final_t.shape[0]
    rows = vec // n

    def peers(count, body):
        if count <= 8:
            for step in range(1, count):
                body(step)
        else:
            pl.loop(1, count)(body)

    def other(step):
        return lax.rem(me + step, n)

    def other_z(step):
        return lax.rem(mz + step, nz)

    def remote(src, dst, send, recv, **where):
        return pltpu.make_async_remote_copy(
            src_ref=src,
            dst_ref=dst,
            send_sem=send,
            recv_sem=recv,
            device_id=where,
            device_id_type=MESH,
        )

    loads = [
        pltpu.make_async_copy(fresh.at[1], fresh_kv.at[0], load_sem.at[0]),
        pltpu.make_async_copy(fresh.at[2], fresh_kv.at[1], load_sem.at[1]),
        pltpu.make_async_copy(out_weight, weight_v, load_sem.at[2]),
        pltpu.make_async_copy(hidden, hidden_v, load_sem.at[3]),
    ]
    own_q = [fresh.at[0, :, pl.ds(h * HEAD_DIM, HEAD_DIM)] for h in range(heads)]
    own_copies = [
        pltpu.make_async_copy(own_q[h], q_all[h].at[me], own_sem.at[h]) for h in range(heads)
    ]
    for copy in loads + own_copies[:slots]:
        copy.start()

    barrier = pltpu.get_barrier_semaphore()
    peers(n, lambda d: pl.semaphore_signal(
        barrier, inc=1, device_id={"patch": other(d)}, device_id_type=MESH))
    peers(nz, lambda d: pl.semaphore_signal(
        barrier, inc=1, device_id={"head": other_z(d)}, device_id_type=MESH))
    pl.semaphore_wait(barrier, n - 1 + nz - 1)

    if n == 8:
        near = me + 1 - 2 * lax.rem(me, 2)
        side = me + 2 - 4 * lax.rem(me // 2, 2)
        over = me + 4 - 8 * (me // 4)
        diag = side + over - me
        half = tok // 2
        low, high = pl.ds(0, half), pl.ds(half, half)
        near_of = lambda p: p + near - me

        def q_copy(h, kind, src, dst, to):
            return remote(src, dst, q_send.at[h, kind], q_recv.at[h, kind], patch=to)

        def first(h):
            dst = q_all[h].at[me]
            return [q_copy(h, k, own_q[h], dst, to) for k, to in ((0, side), (1, over), (2, near))]

        def second(h):
            from_side, from_over = q_all[h].at[side], q_all[h].at[over]
            return [
                q_copy(h, 3, from_side.at[low], from_side.at[low], over),
                q_copy(h, 4, from_over.at[high], from_over.at[high], side),
                q_copy(h, 5, from_side, from_side, near),
                q_copy(h, 6, from_over, from_over, near),
            ]

        def third(h):
            block = q_all[h].at[diag]
            return [q_copy(h, 7, block, block, near)]

        def arrive(h, kind, dst):
            q_copy(h, kind, dst, dst, near).wait_recv()

        def start(copies):
            for copy in copies:
                copy.start()

        def relay(h):
            arrive(h, 0, q_all[h].at[side])
            arrive(h, 1, q_all[h].at[over])
            start(second(h))

        def relay_last(h):
            arrive(h, 3, q_all[h].at[diag].at[low])
            arrive(h, 4, q_all[h].at[diag].at[high])
            start(third(h))

        def before(h):
            if h + 2 < heads:
                start(first(h + 2))
            if h + 1 < heads:
                relay(h + 1)
            relay_last(h)
            arrive(h, 2, q_all[h].at[near])
            arrive(h, 5, q_all[h].at[near_of(side)])
            arrive(h, 6, q_all[h].at[near_of(over)])
            arrive(h, 7, q_all[h].at[near_of(diag)])

        def prologue():
            for h in range(min(2, heads)):
                start(first(h))

        def middle():
            relay(0)

        def refill(h):
            pass

        def sent():
            for h in range(heads):
                for copy in first(h) + second(h) + third(h):
                    copy.wait_send()

    else:

        def direct(h, d):
            return remote(
                own_q[h], q_all[h].at[me], q_send.at[h, d], q_recv.at[h, d], patch=other(d)
            )

        def prologue():
            for h in range(slots):
                peers(n, lambda d: direct(h, d).start())

        def refill(h):
            later = h + slots
            if later < heads:
                peers(n, lambda d: pl.semaphore_signal(
                    free_sem.at[h], inc=1, device_id={"patch": other(d)}, device_id_type=MESH))
                pl.semaphore_wait(free_sem.at[h], n - 1)
                own_copies[later].start()
                peers(n, lambda d: direct(later, d).start())

        def middle():
            pass

        def before(h):
            peers(n, lambda d: direct(h, d).wait_recv())

        def sent():
            for h in range(heads):
                peers(n, lambda d: direct(h, d).wait_send())

    prologue()

    is_mine = [refresh[s] == me for s in range(REFRESH)]
    mine = is_mine[0] | is_mine[1] | is_mine[2] | is_mine[3]
    group = 128
    r, c = iota((2 * group, 2 * group), 0), iota((2 * group, 2 * group), 1)
    unmix = (c == jnp.where(r < group, 2 * r, 2 * (r - group) + 1)).astype(BF16)
    eye = (iota((HEAD_DIM, HEAD_DIM), 0) == iota((HEAD_DIM, HEAD_DIM), 1)).astype(BF16)
    loads[0].wait()
    loads[1].wait()
    for g in range(tok // group):
        at = pl.ds(g * group, group)
        mixed = jnp.dot(unmix, kv[pl.ds(g * group, group)].reshape(2 * group, -1), preferred_element_type=F32)
        mixed = mixed.astype(BF16)
        keys[at, :] = jnp.where(mine, fresh_kv[0, at, :], mixed[:group])
        picked = jnp.where(mine, fresh_kv[1, at, :], mixed[group:])
        for h in range(heads):
            cols = slice(h * HEAD_DIM, (h + 1) * HEAD_DIM)
            values_t[h, :, at] = lax.dot_general(
                eye, picked[:, cols], NT, preferred_element_type=F32
            ).astype(BF16)
    middle()

    k_of = iota((vec, vec), 1)
    r_of = iota((vec, vec), 0)
    row_k = (r_of & (LAT_CH - 1)) * 4 + (r_of >> 5) * 2 + ((r_of >> 4) & 1)
    order = k_of == row_k
    final_rows = jnp.dot(order.astype(BF16), final_t[...], preferred_element_type=F32)
    gated = final_rows * gate[...]
    gated_hi = gated.astype(BF16)
    gated_lo = (gated - gated_hi.astype(F32)).astype(BF16)
    loads[2].wait()
    w2_f = lax.dot_general(
        jnp.concatenate([gated_hi, gated_lo], axis=0), weight_v[...], NT, preferred_element_type=F32
    )
    w2_f = w2_f[:vec] + w2_f[vec:]
    w2_hi = w2_f.astype(BF16)
    w2[:vec, :] = w2_hi
    w2[vec:, :] = (w2_f - w2_hi.astype(F32)).astype(BF16)
    loads[3].wait()
    bias_col = jnp.sum(jnp.where(order, bias[...], 0.0), axis=1, keepdims=True)
    hid_t[...] = bias_col + lax.dot_general(
        final_rows.astype(BF16), hidden_v[...], NT, preferred_element_type=F32
    )
    rr, cc = iota(spread.shape, 0), iota(spread.shape, 1)
    spread[...] = (cc == jnp.where(rr < tok, 2 * rr, 2 * (rr - tok) + 1)).astype(BF16)

    def st_copy(h, d):
        part = stats[h].at[me]
        return remote(part, part, st_send.at[h, d], st_recv.at[h, d], patch=other(d))

    for h in range(heads):
        own_copies[h].wait()
        before(h)
        cols = slice(h * HEAD_DIM, (h + 1) * HEAD_DIM)

        @pl.loop(0, REFRESH, step=2)
        def _(base):
            pair = (base, base + 1)
            scores = [
                lax.dot_general(
                    keys[:, cols], q_all[h][refresh[s]], NT, preferred_element_type=F32
                )
                for s in pair
            ]
            nums = []
            for s, score in zip(pair, scores):
                top = jnp.max(score, axis=0, keepdims=True)
                weights = jnp.exp2((score - top) * SCALE2)
                stats[h][me, pl.ds(s, 1), :] = top
                stats[h][me, pl.ds(s + REFRESH, 1), :] = jnp.sum(weights, axis=0, keepdims=True)
                nums.append(
                    jnp.dot(values_t[h], weights.astype(BF16), preferred_element_type=F32)
                )
            for s, num in zip(pair, nums):
                num_hi = num.astype(BF16)
                num_lo = (num - num_hi.astype(F32)).astype(BF16)
                both = jnp.dot(w2[:, cols], num_hi, preferred_element_type=F32)
                rest = jnp.dot(w2[:vec, cols], num_lo, preferred_element_type=F32)
                u_buf[h, s] = both[:vec] + both[vec:] + rest

        peers(n, lambda d: st_copy(h, d).start())
        refill(h)

    sums = [jnp.zeros((vec, tok), F32) for _ in range(REFRESH)]
    for h in range(heads):
        peers(n, lambda d: st_copy(h, d).wait_recv())
        every = stats[h][...]
        tops, dens = every[:, :REFRESH], every[:, REFRESH:]
        top = jnp.max(tops, axis=0)
        den = jnp.sum(dens * jnp.exp2((tops - top[None]) * SCALE2), axis=0)
        factor = jnp.exp2((stats[h][me][:REFRESH] - top) * SCALE2) / den
        for s in range(REFRESH):
            sums[s] = sums[s] + u_buf[h, s] * factor[s : s + 1]
    for p in range(n):
        for s in range(REFRESH):
            rs_out[p, s] = sums[s][p * rows : (p + 1) * rows]

    def rs_copy(d):
        to = other(d)
        return remote(rs_out.at[to], rs_in.at[d], rs_send.at[d], rs_recv.at[d], patch=to)

    peers(n, lambda d: rs_copy(d).start())
    peers(n, lambda d: rs_copy(d).wait_recv())
    total = rs_out[me]
    for d in range(1, n):
        total = total + rs_in[d]
    z_out[...] = total

    def z_copy(d):
        to = other_z(d)
        return remote(z_out.at[to], z_in.at[d], z_send.at[d], z_recv.at[d], head=to)

    peers(nz, lambda d: z_copy(d).start())
    peers(nz, lambda d: z_copy(d).wait_recv())
    total = z_out[mz]
    for d in range(1, nz):
        total = total + z_in[d]
    z_all[mz] = total

    def zg_copy(d):
        part = z_all.at[mz]
        return remote(part, part, zg_send.at[d], zg_recv.at[d], head=other_z(d))

    peers(nz, lambda d: zg_copy(d).start())
    peers(nz, lambda d: zg_copy(d).wait_recv())
    for p in range(n):
        part = z_all[0]
        for s in range(1, REFRESH):
            part = jnp.where(refresh[s] == p, z_all[s], part)
        ag_out[p] = part

    def ag_copy(d):
        to = other(d)
        return remote(ag_out.at[to], ag.at[me], ag_send.at[d], ag_recv.at[d], patch=to)

    peers(n, lambda d: ag_copy(d).start())
    ag[me] = ag_out[me]
    peers(n, lambda d: ag_copy(d).wait_recv())
    parts = [ag[p] for p in range(n)]
    velocity = jnp.concatenate(parts, axis=0) + hid_t[...]
    wide = [
        jnp.concatenate([velocity[a * 32 : a * 32 + 16], velocity[a * 32 + 16 : a * 32 + 32]], axis=1)
        for a in range(2)
    ]
    wide = jnp.concatenate(wide, axis=0)
    one = wide.astype(BF16)
    left = wide - one.astype(F32)
    two = left.astype(BF16)
    three = (left - two.astype(F32)).astype(BF16)
    pieces = jnp.dot(
        jnp.concatenate([one, two, three], axis=0), spread[...], preferred_element_type=F32
    )
    field = pieces[:32] + pieces[32:64] + pieces[64:]
    for a in range(2):
        fresh_row = field[a * LAT_CH : (a + 1) * LAT_CH]
        row = jnp.where(mine, fresh_row, cache[a].astype(F32))
        latent = noisy[a].astype(F32) - noise[0] * row
        dec[a] = (latent / 0.3611 + 0.1159).astype(BF16)

    after, prior = lax.rem(me + 1, n), lax.rem(me + n - 1, n)
    edges = [
        remote(dec.at[1], halo.at[0], halo_send.at[0], halo_recv.at[0], patch=after),
        remote(dec.at[0], halo.at[1], halo_send.at[1], halo_recv.at[1], patch=prior),
    ]
    for copy in edges:
        copy.start()
    for copy in edges:
        copy.wait_recv()
    lines = [
        jnp.where(me > 0, halo[0].astype(F32), 0.0),
        dec[0].astype(F32),
        dec[1].astype(F32),
        jnp.where(me < n - 1, halo[1].astype(F32), 0.0),
    ]
    width = dec.shape[2]
    column = iota((LAT_CH, width), 1)
    shifted = []
    for line in lines:
        before_it = jnp.where(column == 0, 0.0, pltpu.roll(line, 1, 1))
        after_it = jnp.where(column == width - 1, 0.0, pltpu.roll(line, width - 1, 1))
        shifted.append([x.astype(BF16) for x in (before_it, line, after_it)])
    conv_col = to_column(conv_bias[...])
    for a in range(2):
        stencil = jnp.concatenate([shifted[a + u][v] for u in range(3) for v in range(3)], axis=0)
        result = lax.dot_general(conv_t[...], stencil, TN, preferred_element_type=F32)
        out[a] = (result + conv_col).astype(BF16)

    sent()
    for h in range(heads):
        peers(n, lambda d: st_copy(h, d).wait_send())
    peers(n, lambda d: rs_copy(d).wait_send())
    peers(nz, lambda d: z_copy(d).wait_send())
    peers(nz, lambda d: zg_copy(d).wait_send())
    peers(n, lambda d: ag_copy(d).wait_send())
    for copy in edges:
        copy.wait_send()


def on_device(
    n,
    nz,
    fresh_qkv,
    kv_cache,
    hidden,
    refresh,
    out_weight,
    final_weight,
    final_bias,
    gate_scale,
    noise_level,
    noisy_latent,
    velocity_cache,
    conv_weight,
    conv_bias,
):
    tok, _, local = fresh_qkv.shape
    heads = local // HEAD_DIM
    depth, vec = final_weight.shape
    rows = vec // n
    assert nz == REFRESH
    width = noisy_latent.shape[2]
    channels = conv_weight.shape[0]
    vmem, smem, anyw = (pl.BlockSpec(memory_space=m) for m in (pltpu.VMEM, pltpu.SMEM, pl.ANY))
    dma = pltpu.SemaphoreType.DMA
    kinds = 8 if n == 8 else n
    scratch = (
        [pltpu.VMEM((n, tok, HEAD_DIM), BF16)] * q_slots(n, heads)
        + [pltpu.VMEM((n, 2 * REFRESH, tok), F32)] * heads
        + [
            pltpu.VMEM((2, tok, local), BF16),
            pltpu.VMEM((tok, depth), BF16),
            pltpu.VMEM((local, depth), BF16),
            pltpu.VMEM((tok, local), BF16),
            pltpu.VMEM((heads, HEAD_DIM, tok), BF16),
            pltpu.VMEM((2 * vec, local), BF16),
            pltpu.VMEM((heads, REFRESH, vec, tok), F32),
            pltpu.VMEM((2 * tok, 2 * tok), BF16),
            pltpu.VMEM((vec, tok), F32),
            pltpu.VMEM((n, REFRESH, rows, tok), F32),
            pltpu.VMEM((n, REFRESH, rows, tok), F32),
            pltpu.VMEM((nz, rows, tok), F32),
            pltpu.VMEM((nz, rows, tok), F32),
            pltpu.VMEM((nz, rows, tok), F32),
            pltpu.VMEM((n, rows, tok), F32),
            pltpu.VMEM((n, rows, tok), F32),
            pltpu.VMEM((2, LAT_CH, width), BF16),
            pltpu.VMEM((2, LAT_CH, width), BF16),
            dma((4,)),
            dma((heads,)),
            dma((heads, kinds)),
            dma((heads, kinds)),
            dma((heads, n)),
            dma((heads, n)),
            dma((n,)),
            dma((n,)),
            dma((nz,)),
            dma((nz,)),
            dma((nz,)),
            dma((nz,)),
            dma((n,)),
            dma((n,)),
            dma((2,)),
            dma((2,)),
            pltpu.SemaphoreType.REGULAR((heads,)),
        ]
    )
    return pl.pallas_call(
        functools.partial(kernel, n, nz, heads, tok),
        out_shape=jax.ShapeDtypeStruct((2, channels, width), BF16),
        in_specs=[smem, smem, anyw, vmem, anyw, anyw] + [vmem] * 7,
        out_specs=vmem,
        scratch_shapes=scratch,
        compiler_params=pltpu.CompilerParams(
            collective_id=0, has_side_effects=True, vmem_limit_bytes=58 * 1024 * 1024
        ),
    )(
        refresh,
        noise_level,
        jnp.transpose(fresh_qkv, (1, 0, 2)),
        kv_cache,
        hidden,
        out_weight,
        final_weight.T,
        final_bias[None, :],
        gate_scale[None, :],
        noisy_latent,
        velocity_cache,
        jnp.transpose(conv_weight, (1, 2, 3, 0)).reshape(-1, channels),
        conv_bias[None, :],
    )


def solution(mesh):
    return jax.shard_map(
        functools.partial(on_device, mesh.shape["patch"], mesh.shape["head"]),
        mesh=mesh,
        in_specs=(
            P("patch", None, "head"),
            P("patch", None, "head"),
            P("patch", None),
            P(),
            P("head", None),
            P(),
            P(),
            P(),
            P(),
            P("patch", None, None),
            P("patch", None, None),
            P("head", None, None, None),
            P("head"),
        ),
        out_specs=P("patch", "head", None),
        check_vma=False,
    )
```

```python
import functools
import math

import jax
import jax.numpy as jnp
from jax import lax
from jax.experimental import pallas as pl
from jax.experimental.pallas import tpu as pltpu
from jax.sharding import PartitionSpec as P

HEAD_DIM = 128
LAT_CH = 16
REFRESH = 4
MESH = pl.DeviceIdType.MESH
SCALE2 = math.log2(math.e) / math.sqrt(HEAD_DIM)
NT = (((1,), (1,)), ((), ()))
TN = (((0,), (0,)), ((), ()))
F32 = jnp.float32
BF16 = jnp.bfloat16


def iota(shape, dim):
    return lax.broadcasted_iota(jnp.int32, shape, dim)


def q_slots(n, heads):
    return heads if n == 8 else min(2, heads)


def to_column(row):
    size = row.shape[1]
    eye = iota((size, size), 0) == iota((size, size), 1)
    return jnp.sum(jnp.where(eye, row, 0.0), axis=1, keepdims=True)


def kernel(
    n,
    nz,
    heads,
    tok,
    refresh,
    noise,
    fresh,
    kv,
    hidden,
    out_weight,
    final_t,
    bias,
    gate,
    noisy,
    cache,
    conv_t,
    conv_bias,
    out,
    *scratch,
):
    slots = q_slots(n, heads)
    q_all = [scratch[h % slots] for h in range(heads)]
    stats = scratch[slots : slots + heads]
    chips = scratch[slots + heads : slots + 2 * heads]
    (
        fresh_kv,
        hidden_v,
        weight_v,
        keys,
        values_t,
        w2,
        u_buf,
        spread,
        hid_t,
        rs_out,
        rs_in,
        z_out,
        z_in,
        z_all,
        ag_out,
        ag,
        dec,
        halo,
        load_sem,
        own_sem,
        q_send,
        q_recv,
        st_send,
        st_recv,
        rs_send,
        rs_recv,
        z_send,
        z_recv,
        zg_send,
        zg_recv,
        ag_send,
        ag_recv,
        halo_send,
        halo_recv,
        free_sem,
    ) = scratch[slots + 2 * heads :]
    me = lax.axis_index("patch")
    mz = lax.axis_index("head")
    vec = final_t.shape[0]
    rows = vec // n

    def peers(count, body):
        if count <= 8:
            for step in range(1, count):
                body(step)
        else:
            pl.loop(1, count)(body)

    def other(step):
        return lax.rem(me + step, n)

    def other_z(step):
        return lax.rem(mz + step, nz)

    def remote(src, dst, send, recv, **where):
        return pltpu.make_async_remote_copy(
            src_ref=src,
            dst_ref=dst,
            send_sem=send,
            recv_sem=recv,
            device_id=where,
            device_id_type=MESH,
        )

    loads = [
        pltpu.make_async_copy(fresh.at[1], fresh_kv.at[0], load_sem.at[0]),
        pltpu.make_async_copy(fresh.at[2], fresh_kv.at[1], load_sem.at[1]),
        pltpu.make_async_copy(out_weight, weight_v, load_sem.at[2]),
        pltpu.make_async_copy(hidden, hidden_v, load_sem.at[3]),
    ]
    own_q = [fresh.at[0, :, pl.ds(h * HEAD_DIM, HEAD_DIM)] for h in range(heads)]
    own_copies = [
        pltpu.make_async_copy(own_q[h], q_all[h].at[me], own_sem.at[h]) for h in range(heads)
    ]
    for copy in loads + own_copies[:slots]:
        copy.start()

    barrier = pltpu.get_barrier_semaphore()
    peers(n, lambda d: pl.semaphore_signal(
        barrier, inc=1, device_id={"patch": other(d)}, device_id_type=MESH))
    peers(nz, lambda d: pl.semaphore_signal(
        barrier, inc=1, device_id={"head": other_z(d)}, device_id_type=MESH))
    pl.semaphore_wait(barrier, n - 1 + nz - 1)

    def st_copy(h, d):
        part = stats[h].at[me]
        return remote(part, part, st_send.at[h, d], st_recv.at[h, d], patch=other(d))

    if n == 8:
        near = me + 1 - 2 * lax.rem(me, 2)
        side = me + 2 - 4 * lax.rem(me // 2, 2)
        over = me + 4 - 8 * (me // 4)
        diag = side + over - me
        half = tok // 2
        low, high = pl.ds(0, half), pl.ds(half, half)
        near_of = lambda p: p + near - me

        def q_copy(h, kind, src, dst, to):
            return remote(src, dst, q_send.at[h, kind], q_recv.at[h, kind], patch=to)

        def first(h):
            dst = q_all[h].at[me]
            return [q_copy(h, k, own_q[h], dst, to) for k, to in ((0, side), (1, over), (2, near))]

        def second(h):
            from_side, from_over = q_all[h].at[side], q_all[h].at[over]
            return [
                q_copy(h, 3, from_side.at[low], from_side.at[low], over),
                q_copy(h, 4, from_over.at[high], from_over.at[high], side),
                q_copy(h, 5, from_side, from_side, near),
                q_copy(h, 6, from_over, from_over, near),
            ]

        def third(h):
            block = q_all[h].at[diag]
            return [q_copy(h, 7, block, block, near)]

        def arrive(h, kind, dst):
            q_copy(h, kind, dst, dst, near).wait_recv()

        def start(copies):
            for copy in copies:
                copy.start()

        def relay(h):
            arrive(h, 0, q_all[h].at[side])
            arrive(h, 1, q_all[h].at[over])
            start(second(h))

        def relay_last(h):
            arrive(h, 3, q_all[h].at[diag].at[low])
            arrive(h, 4, q_all[h].at[diag].at[high])
            start(third(h))

        def before(h):
            arrive(h, 2, q_all[h].at[near])
            arrive(h, 5, q_all[h].at[near_of(side)])
            arrive(h, 6, q_all[h].at[near_of(over)])
            arrive(h, 7, q_all[h].at[near_of(diag)])

        def between(h):
            if h + 1 < heads:
                relay_last(h + 1)
            if h + 2 < heads:
                relay(h + 2)
            if h + 3 < heads:
                start(first(h + 3))
            if h >= 1:
                chip_stats(h - 1)

        def chip_copies(h):
            part = chips[h].at[me // 2]
            return [
                remote(part, part, st_send.at[h, k], st_recv.at[h, k], patch=to)
                for k, to in ((1, side), (2, over), (3, diag))
            ]

        def chip_stats(h):
            near_copy(h).wait_recv()
            both = (stats[h][me], stats[h][near])
            tops = [x[:REFRESH] for x in both]
            top = jnp.maximum(*tops)
            den = sum(x[REFRESH:] * jnp.exp2((x[:REFRESH] - top) * SCALE2) for x in both)
            chips[h][me // 2, :REFRESH] = top
            chips[h][me // 2, REFRESH:] = den
            start(chip_copies(h))

        def near_copy(h):
            part = stats[h].at[me]
            return remote(part, part, st_send.at[h, 0], st_recv.at[h, 0], patch=near)

        def publish(h):
            if h < heads - 1:
                near_copy(h).start()
            else:
                peers(n, lambda d: st_copy(h, d).start())

        def collect(h):
            if h < heads - 1:
                for copy in chip_copies(h):
                    copy.wait_recv()
                return chips[h][...]
            peers(n, lambda d: st_copy(h, d).wait_recv())
            return stats[h][...]

        def published(h):
            if h < heads - 1:
                near_copy(h).wait_send()
                for copy in chip_copies(h):
                    copy.wait_send()
            else:
                peers(n, lambda d: st_copy(h, d).wait_send())

        def prologue():
            start(first(0))

        def middle(part):
            if part == 0:
                relay(0)
                if heads > 1:
                    start(first(1))
            else:
                relay_last(0)
                if heads > 1:
                    relay(1)
                if heads > 2:
                    start(first(2))

        def refill(h):
            pass

        def sent():
            for h in range(heads):
                for copy in first(h) + second(h) + third(h):
                    copy.wait_send()

    else:

        def direct(h, d):
            return remote(
                own_q[h], q_all[h].at[me], q_send.at[h, d], q_recv.at[h, d], patch=other(d)
            )

        def prologue():
            for h in range(slots):
                peers(n, lambda d: direct(h, d).start())

        def refill(h):
            later = h + slots
            if later < heads:
                peers(n, lambda d: pl.semaphore_signal(
                    free_sem.at[h], inc=1, device_id={"patch": other(d)}, device_id_type=MESH))
                pl.semaphore_wait(free_sem.at[h], n - 1)
                own_copies[later].start()
                peers(n, lambda d: direct(later, d).start())

        def middle(part):
            pass

        def between(h):
            pass

        def publish(h):
            peers(n, lambda d: st_copy(h, d).start())

        def collect(h):
            peers(n, lambda d: st_copy(h, d).wait_recv())
            return stats[h][...]

        def published(h):
            peers(n, lambda d: st_copy(h, d).wait_send())

        def before(h):
            peers(n, lambda d: direct(h, d).wait_recv())

        def sent():
            for h in range(heads):
                peers(n, lambda d: direct(h, d).wait_send())

    prologue()

    is_mine = [refresh[s] == me for s in range(REFRESH)]
    mine = is_mine[0] | is_mine[1] | is_mine[2] | is_mine[3]
    group = 128
    r, c = iota((2 * group, 2 * group), 0), iota((2 * group, 2 * group), 1)
    unmix = (c == jnp.where(r < group, 2 * r, 2 * (r - group) + 1)).astype(BF16)
    eye = (iota((HEAD_DIM, HEAD_DIM), 0) == iota((HEAD_DIM, HEAD_DIM), 1)).astype(BF16)
    loads[0].wait()
    loads[1].wait()
    for g in range(tok // group):
        at = pl.ds(g * group, group)
        mixed = jnp.dot(unmix, kv[pl.ds(g * group, group)].reshape(2 * group, -1), preferred_element_type=F32)
        mixed = mixed.astype(BF16)
        keys[at, :] = jnp.where(mine, fresh_kv[0, at, :], mixed[:group])
        picked = jnp.where(mine, fresh_kv[1, at, :], mixed[group:])
        for h in range(heads):
            cols = slice(h * HEAD_DIM, (h + 1) * HEAD_DIM)
            values_t[h, :, at] = lax.dot_general(
                eye, picked[:, cols], NT, preferred_element_type=F32
            ).astype(BF16)
    middle(0)

    k_of = iota((vec, vec), 1)
    r_of = iota((vec, vec), 0)
    row_k = (r_of & (LAT_CH - 1)) * 4 + (r_of >> 5) * 2 + ((r_of >> 4) & 1)
    order = k_of == row_k
    final_rows = jnp.dot(order.astype(BF16), final_t[...], preferred_element_type=F32)
    gated = final_rows * gate[...]
    gated_hi = gated.astype(BF16)
    gated_lo = (gated - gated_hi.astype(F32)).astype(BF16)
    loads[2].wait()
    w2_f = lax.dot_general(
        jnp.concatenate([gated_hi, gated_lo], axis=0), weight_v[...], NT, preferred_element_type=F32
    )
    w2_f = w2_f[:vec] + w2_f[vec:]
    w2_hi = w2_f.astype(BF16)
    w2[:vec, :] = w2_hi
    w2[vec:, :] = (w2_f - w2_hi.astype(F32)).astype(BF16)
    middle(1)
    loads[3].wait()
    bias_col = jnp.sum(jnp.where(order, bias[...], 0.0), axis=1, keepdims=True)
    hid_t[...] = bias_col + lax.dot_general(
        final_rows.astype(BF16), hidden_v[...], NT, preferred_element_type=F32
    )
    rr, cc = iota(spread.shape, 0), iota(spread.shape, 1)
    spread[...] = (cc == jnp.where(rr < tok, 2 * rr, 2 * (rr - tok) + 1)).astype(BF16)

    for h in range(heads):
        own_copies[h].wait()
        before(h)
        cols = slice(h * HEAD_DIM, (h + 1) * HEAD_DIM)

        @pl.loop(0, REFRESH, step=2)
        def _(base):
            pair = (base, base + 1)
            scores = [
                lax.dot_general(
                    keys[:, cols], q_all[h][refresh[s]], NT, preferred_element_type=F32
                )
                for s in pair
            ]
            nums = []
            for s, score in zip(pair, scores):
                top = jnp.max(score, axis=0, keepdims=True)
                weights = jnp.exp2((score - top) * SCALE2)
                stats[h][me, pl.ds(s, 1), :] = top
                stats[h][me, pl.ds(s + REFRESH, 1), :] = jnp.sum(weights, axis=0, keepdims=True)
                nums.append(
                    jnp.dot(values_t[h], weights.astype(BF16), preferred_element_type=F32)
                )
            for s, num in zip(pair, nums):
                num_hi = num.astype(BF16)
                num_lo = (num - num_hi.astype(F32)).astype(BF16)
                both = jnp.dot(w2[:, cols], num_hi, preferred_element_type=F32)
                rest = jnp.dot(w2[:vec, cols], num_lo, preferred_element_type=F32)
                u_buf[h, s] = both[:vec] + both[vec:] + rest

            pl.when(base == 0)(functools.partial(between, h))

        publish(h)
        refill(h)

    sums = [jnp.zeros((vec, tok), F32) for _ in range(REFRESH)]
    for h in range(heads):
        every = collect(h)
        tops, dens = every[:, :REFRESH], every[:, REFRESH:]
        top = jnp.max(tops, axis=0)
        den = jnp.sum(dens * jnp.exp2((tops - top[None]) * SCALE2), axis=0)
        factor = jnp.exp2((stats[h][me][:REFRESH] - top) * SCALE2) / den
        for s in range(REFRESH):
            sums[s] = sums[s] + u_buf[h, s] * factor[s : s + 1]
    for p in range(n):
        for s in range(REFRESH):
            rs_out[p, s] = sums[s][p * rows : (p + 1) * rows]

    def rs_copy(d):
        to = other(d)
        return remote(rs_out.at[to], rs_in.at[d], rs_send.at[d], rs_recv.at[d], patch=to)

    peers(n, lambda d: rs_copy(d).start())
    peers(n, lambda d: rs_copy(d).wait_recv())
    total = rs_out[me]
    for d in range(1, n):
        total = total + rs_in[d]
    z_out[...] = total

    def z_copy(d):
        to = other_z(d)
        return remote(z_out.at[to], z_in.at[d], z_send.at[d], z_recv.at[d], head=to)

    peers(nz, lambda d: z_copy(d).start())
    peers(nz, lambda d: z_copy(d).wait_recv())
    total = z_out[mz]
    for d in range(1, nz):
        total = total + z_in[d]
    z_all[mz] = total

    def zg_copy(d):
        part = z_all.at[mz]
        return remote(part, part, zg_send.at[d], zg_recv.at[d], head=other_z(d))

    peers(nz, lambda d: zg_copy(d).start())
    peers(nz, lambda d: zg_copy(d).wait_recv())
    for p in range(n):
        part = z_all[0]
        for s in range(1, REFRESH):
            part = jnp.where(refresh[s] == p, z_all[s], part)
        ag_out[p] = part

    def ag_copy(d):
        to = other(d)
        return remote(ag_out.at[to], ag.at[me], ag_send.at[d], ag_recv.at[d], patch=to)

    peers(n, lambda d: ag_copy(d).start())
    ag[me] = ag_out[me]
    peers(n, lambda d: ag_copy(d).wait_recv())
    parts = [ag[p] for p in range(n)]
    velocity = jnp.concatenate(parts, axis=0) + hid_t[...]
    wide = [
        jnp.concatenate([velocity[a * 32 : a * 32 + 16], velocity[a * 32 + 16 : a * 32 + 32]], axis=1)
        for a in range(2)
    ]
    wide = jnp.concatenate(wide, axis=0)
    one = wide.astype(BF16)
    left = wide - one.astype(F32)
    two = left.astype(BF16)
    three = (left - two.astype(F32)).astype(BF16)
    pieces = jnp.dot(
        jnp.concatenate([one, two, three], axis=0), spread[...], preferred_element_type=F32
    )
    field = pieces[:32] + pieces[32:64] + pieces[64:]
    for a in range(2):
        fresh_row = field[a * LAT_CH : (a + 1) * LAT_CH]
        row = jnp.where(mine, fresh_row, cache[a].astype(F32))
        latent = noisy[a].astype(F32) - noise[0] * row
        dec[a] = (latent / 0.3611 + 0.1159).astype(BF16)

    after, prior = lax.rem(me + 1, n), lax.rem(me + n - 1, n)
    edges = [
        remote(dec.at[1], halo.at[0], halo_send.at[0], halo_recv.at[0], patch=after),
        remote(dec.at[0], halo.at[1], halo_send.at[1], halo_recv.at[1], patch=prior),
    ]
    for copy in edges:
        copy.start()
    for copy in edges:
        copy.wait_recv()
    lines = [
        jnp.where(me > 0, halo[0].astype(F32), 0.0),
        dec[0].astype(F32),
        dec[1].astype(F32),
        jnp.where(me < n - 1, halo[1].astype(F32), 0.0),
    ]
    width = dec.shape[2]
    column = iota((LAT_CH, width), 1)
    shifted = []
    for line in lines:
        before_it = jnp.where(column == 0, 0.0, pltpu.roll(line, 1, 1))
        after_it = jnp.where(column == width - 1, 0.0, pltpu.roll(line, width - 1, 1))
        shifted.append([x.astype(BF16) for x in (before_it, line, after_it)])
    conv_col = to_column(conv_bias[...])
    for a in range(2):
        stencil = jnp.concatenate([shifted[a + u][v] for u in range(3) for v in range(3)], axis=0)
        result = lax.dot_general(conv_t[...], stencil, TN, preferred_element_type=F32)
        out[a] = (result + conv_col).astype(BF16)

    sent()
    for h in range(heads):
        published(h)
    peers(n, lambda d: rs_copy(d).wait_send())
    peers(nz, lambda d: z_copy(d).wait_send())
    peers(nz, lambda d: zg_copy(d).wait_send())
    peers(n, lambda d: ag_copy(d).wait_send())
    for copy in edges:
        copy.wait_send()


def on_device(
    n,
    nz,
    fresh_qkv,
    kv_cache,
    hidden,
    refresh,
    out_weight,
    final_weight,
    final_bias,
    gate_scale,
    noise_level,
    noisy_latent,
    velocity_cache,
    conv_weight,
    conv_bias,
):
    tok, _, local = fresh_qkv.shape
    heads = local // HEAD_DIM
    depth, vec = final_weight.shape
    rows = vec // n
    assert nz == REFRESH
    width = noisy_latent.shape[2]
    channels = conv_weight.shape[0]
    vmem, smem, anyw = (pl.BlockSpec(memory_space=m) for m in (pltpu.VMEM, pltpu.SMEM, pl.ANY))
    dma = pltpu.SemaphoreType.DMA
    kinds = 8 if n == 8 else n
    scratch = (
        [pltpu.VMEM((n, tok, HEAD_DIM), BF16)] * q_slots(n, heads)
        + [pltpu.VMEM((n, 2 * REFRESH, tok), F32)] * heads
        + [pltpu.VMEM((max(n // 2, 1), 2 * REFRESH, tok), F32)] * heads
        + [
            pltpu.VMEM((2, tok, local), BF16),
            pltpu.VMEM((tok, depth), BF16),
            pltpu.VMEM((local, depth), BF16),
            pltpu.VMEM((tok, local), BF16),
            pltpu.VMEM((heads, HEAD_DIM, tok), BF16),
            pltpu.VMEM((2 * vec, local), BF16),
            pltpu.VMEM((heads, REFRESH, vec, tok), F32),
            pltpu.VMEM((2 * tok, 2 * tok), BF16),
            pltpu.VMEM((vec, tok), F32),
            pltpu.VMEM((n, REFRESH, rows, tok), F32),
            pltpu.VMEM((n, REFRESH, rows, tok), F32),
            pltpu.VMEM((nz, rows, tok), F32),
            pltpu.VMEM((nz, rows, tok), F32),
            pltpu.VMEM((nz, rows, tok), F32),
            pltpu.VMEM((n, rows, tok), F32),
            pltpu.VMEM((n, rows, tok), F32),
            pltpu.VMEM((2, LAT_CH, width), BF16),
            pltpu.VMEM((2, LAT_CH, width), BF16),
            dma((4,)),
            dma((heads,)),
            dma((heads, kinds)),
            dma((heads, kinds)),
            dma((heads, n)),
            dma((heads, n)),
            dma((n,)),
            dma((n,)),
            dma((nz,)),
            dma((nz,)),
            dma((nz,)),
            dma((nz,)),
            dma((n,)),
            dma((n,)),
            dma((2,)),
            dma((2,)),
            pltpu.SemaphoreType.REGULAR((heads,)),
        ]
    )
    return pl.pallas_call(
        functools.partial(kernel, n, nz, heads, tok),
        out_shape=jax.ShapeDtypeStruct((2, channels, width), BF16),
        in_specs=[smem, smem, anyw, vmem, anyw, anyw] + [vmem] * 7,
        out_specs=vmem,
        scratch_shapes=scratch,
        compiler_params=pltpu.CompilerParams(
            collective_id=0, has_side_effects=True, vmem_limit_bytes=58 * 1024 * 1024
        ),
    )(
        refresh,
        noise_level,
        jnp.transpose(fresh_qkv, (1, 0, 2)),
        kv_cache,
        hidden,
        out_weight,
        final_weight.T,
        final_bias[None, :],
        gate_scale[None, :],
        noisy_latent,
        velocity_cache,
        jnp.transpose(conv_weight, (1, 2, 3, 0)).reshape(-1, channels),
        conv_bias[None, :],
    )


def solution(mesh):
    return jax.shard_map(
        functools.partial(on_device, mesh.shape["patch"], mesh.shape["head"]),
        mesh=mesh,
        in_specs=(
            P("patch", None, "head"),
            P("patch", None, "head"),
            P("patch", None),
            P(),
            P("head", None),
            P(),
            P(),
            P(),
            P(),
            P("patch", None, None),
            P("patch", None, None),
            P("head", None, None, None),
            P("head"),
        ),
        out_specs=P("patch", "head", None),
        check_vma=False,
    )
```

```python
import functools
import math

import jax
import jax.numpy as jnp
from jax import lax
from jax.experimental import pallas as pl
from jax.experimental.pallas import tpu as pltpu
from jax.sharding import PartitionSpec as P

HEAD_DIM = 128
LAT_CH = 16
REFRESH = 4
MESH = pl.DeviceIdType.MESH
SCALE = 1.0 / math.sqrt(HEAD_DIM)
NT = (((1,), (1,)), ((), ()))
TN = (((0,), (0,)), ((), ()))
F32 = jnp.float32
BF16 = jnp.bfloat16


def iota(shape, dim):
    return lax.broadcasted_iota(jnp.int32, shape, dim)


def q_slots(n, heads):
    return heads if n == 8 else min(2, heads)


def to_column(row):
    size = row.shape[1]
    eye = iota((size, size), 0) == iota((size, size), 1)
    return jnp.sum(jnp.where(eye, row, 0.0), axis=1, keepdims=True)


def kernel(
    n,
    nz,
    heads,
    tok,
    refresh,
    noise,
    fresh,
    kv,
    hidden,
    out_weight,
    final_t,
    bias,
    gate,
    noisy,
    cache,
    conv_t,
    conv_bias,
    out,
    *scratch,
):
    slots = q_slots(n, heads)
    q_all = [scratch[h % slots] for h in range(heads)]
    stats = scratch[slots : slots + heads]
    chips = scratch[slots + heads : slots + 2 * heads]
    (
        fresh_kv,
        hidden_v,
        weight_v,
        keys,
        values_t,
        w2,
        u_buf,
        spread,
        hid_t,
        rows_t,
        rs_out,
        rs_in,
        z_out,
        z_in,
        z_all,
        ag_out,
        ag,
        dec,
        halo,
        load_sem,
        own_sem,
        q_send,
        q_recv,
        st_send,
        st_recv,
        rs_send,
        rs_recv,
        z_send,
        z_recv,
        zg_send,
        zg_recv,
        ag_send,
        ag_recv,
        halo_send,
        halo_recv,
        free_sem,
    ) = scratch[slots + 2 * heads :]
    me = lax.axis_index("patch")
    mz = lax.axis_index("head")
    vec = final_t.shape[0]
    rows = vec // n

    def peers(count, body):
        if count <= 8:
            for step in range(1, count):
                body(step)
        else:
            pl.loop(1, count)(body)

    def other(step):
        return lax.rem(me + step, n)

    def other_z(step):
        return lax.rem(mz + step, nz)

    def remote(src, dst, send, recv, **where):
        return pltpu.make_async_remote_copy(
            src_ref=src,
            dst_ref=dst,
            send_sem=send,
            recv_sem=recv,
            device_id=where,
            device_id_type=MESH,
        )

    loads = [
        pltpu.make_async_copy(fresh.at[1], fresh_kv.at[0], load_sem.at[0]),
        pltpu.make_async_copy(fresh.at[2], fresh_kv.at[1], load_sem.at[1]),
        pltpu.make_async_copy(out_weight, weight_v, load_sem.at[2]),
        pltpu.make_async_copy(hidden, hidden_v, load_sem.at[3]),
    ]
    own_q = [fresh.at[0, :, pl.ds(h * HEAD_DIM, HEAD_DIM)] for h in range(heads)]
    own_copies = [
        pltpu.make_async_copy(own_q[h], q_all[h].at[me], own_sem.at[h]) for h in range(heads)
    ]
    for copy in loads + own_copies[:slots]:
        copy.start()

    barrier = pltpu.get_barrier_semaphore()
    peers(n, lambda d: pl.semaphore_signal(
        barrier, inc=1, device_id={"patch": other(d)}, device_id_type=MESH))
    peers(nz, lambda d: pl.semaphore_signal(
        barrier, inc=1, device_id={"head": other_z(d)}, device_id_type=MESH))
    pl.semaphore_wait(barrier, n - 1 + nz - 1)

    def st_copy(h, d):
        part = stats[h].at[me]
        return remote(part, part, st_send.at[h, d], st_recv.at[h, d], patch=other(d))

    if n == 8:
        near = me + 1 - 2 * lax.rem(me, 2)
        side = me + 2 - 4 * lax.rem(me // 2, 2)
        over = me + 4 - 8 * (me // 4)
        diag = side + over - me
        half = tok // 2
        low, high = pl.ds(0, half), pl.ds(half, half)
        near_of = lambda p: p + near - me

        def q_copy(h, kind, src, dst, to):
            return remote(src, dst, q_send.at[h, kind], q_recv.at[h, kind], patch=to)

        def first(h):
            dst = q_all[h].at[me]
            return [q_copy(h, k, own_q[h], dst, to) for k, to in ((0, side), (1, over), (2, near))]

        def second(h):
            from_side, from_over = q_all[h].at[side], q_all[h].at[over]
            return [
                q_copy(h, 3, from_side.at[low], from_side.at[low], over),
                q_copy(h, 4, from_over.at[high], from_over.at[high], side),
                q_copy(h, 5, from_side, from_side, near),
                q_copy(h, 6, from_over, from_over, near),
            ]

        def third(h):
            block = q_all[h].at[diag]
            return [q_copy(h, 7, block, block, near)]

        def arrive(h, kind, dst):
            q_copy(h, kind, dst, dst, near).wait_recv()

        def start(copies):
            for copy in copies:
                copy.start()

        def relay(h):
            arrive(h, 0, q_all[h].at[side])
            arrive(h, 1, q_all[h].at[over])
            start(second(h))

        def relay_last(h):
            arrive(h, 3, q_all[h].at[diag].at[low])
            arrive(h, 4, q_all[h].at[diag].at[high])
            start(third(h))

        def before(h):
            arrive(h, 2, q_all[h].at[near])
            arrive(h, 5, q_all[h].at[near_of(side)])
            arrive(h, 6, q_all[h].at[near_of(over)])
            arrive(h, 7, q_all[h].at[near_of(diag)])

        def between(h):
            if h + 1 < heads:
                relay_last(h + 1)
            if h + 2 < heads:
                relay(h + 2)
            if h + 5 < heads:
                start(first(h + 5))
            if h >= 1:
                chip_stats(h - 1)

        def chip_copies(h):
            part = chips[h].at[me // 2]
            return [
                remote(part, part, st_send.at[h, k], st_recv.at[h, k], patch=to)
                for k, to in ((1, side), (2, over), (3, diag))
            ]

        def chip_stats(h):
            near_copy(h).wait_recv()
            both = (stats[h][me], stats[h][near])
            tops = [x[:REFRESH] for x in both]
            top = jnp.maximum(*tops)
            den = sum(x[REFRESH:] * jnp.exp((x[:REFRESH] - top) * SCALE) for x in both)
            chips[h][me // 2, :REFRESH] = top
            chips[h][me // 2, REFRESH:] = den
            start(chip_copies(h))

        def near_copy(h):
            part = stats[h].at[me]
            return remote(part, part, st_send.at[h, 0], st_recv.at[h, 0], patch=near)

        def publish(h):
            if h < heads - 1:
                near_copy(h).start()
            else:
                peers(n, lambda d: st_copy(h, d).start())

        def collect(h):
            if h < heads - 1:
                for copy in chip_copies(h):
                    copy.wait_recv()
                return chips[h][...]
            peers(n, lambda d: st_copy(h, d).wait_recv())
            return stats[h][...]

        def published(h):
            if h < heads - 1:
                near_copy(h).wait_send()
                for copy in chip_copies(h):
                    copy.wait_send()
            else:
                peers(n, lambda d: st_copy(h, d).wait_send())

        def prologue():
            for h in range(min(3, heads)):
                start(first(h))

        def middle(part):
            if part == 0:
                relay(0)
                if heads > 3:
                    start(first(3))
            else:
                relay_last(0)
                if heads > 1:
                    relay(1)
                if heads > 4:
                    start(first(4))

        def refill(h):
            pass

        def sent():
            for h in range(heads):
                for copy in first(h) + second(h) + third(h):
                    copy.wait_send()

    else:

        def direct(h, d):
            return remote(
                own_q[h], q_all[h].at[me], q_send.at[h, d], q_recv.at[h, d], patch=other(d)
            )

        def prologue():
            for h in range(slots):
                peers(n, lambda d: direct(h, d).start())

        def refill(h):
            later = h + slots
            if later < heads:
                peers(n, lambda d: pl.semaphore_signal(
                    free_sem.at[h], inc=1, device_id={"patch": other(d)}, device_id_type=MESH))
                pl.semaphore_wait(free_sem.at[h], n - 1)
                own_copies[later].start()
                peers(n, lambda d: direct(later, d).start())

        def middle(part):
            pass

        def between(h):
            pass

        def publish(h):
            peers(n, lambda d: st_copy(h, d).start())

        def collect(h):
            peers(n, lambda d: st_copy(h, d).wait_recv())
            return stats[h][...]

        def published(h):
            peers(n, lambda d: st_copy(h, d).wait_send())

        def before(h):
            peers(n, lambda d: direct(h, d).wait_recv())

        def sent():
            for h in range(heads):
                peers(n, lambda d: direct(h, d).wait_send())

    prologue()

    is_mine = [refresh[s] == me for s in range(REFRESH)]
    mine = is_mine[0] | is_mine[1] | is_mine[2] | is_mine[3]
    group = 128
    r, c = iota((2 * group, 2 * group), 0), iota((2 * group, 2 * group), 1)
    unmix = (c == jnp.where(r < group, 2 * r, 2 * (r - group) + 1)).astype(BF16)
    eye = (iota((HEAD_DIM, HEAD_DIM), 0) == iota((HEAD_DIM, HEAD_DIM), 1)).astype(BF16)
    loads[0].wait()
    loads[1].wait()
    for g in range(tok // group):
        at = pl.ds(g * group, group)
        mixed = jnp.dot(unmix, kv[pl.ds(g * group, group)].reshape(2 * group, -1), preferred_element_type=F32)
        mixed = mixed.astype(BF16)
        keys[at, :] = jnp.where(mine, fresh_kv[0, at, :], mixed[:group])
        picked = jnp.where(mine, fresh_kv[1, at, :], mixed[group:])
        for h in range(heads):
            cols = slice(h * HEAD_DIM, (h + 1) * HEAD_DIM)
            values_t[h, :, at] = lax.dot_general(
                eye, picked[:, cols], NT, preferred_element_type=F32
            ).astype(BF16)
    middle(0)

    k_of = iota((vec, vec), 1)
    r_of = iota((vec, vec), 0)
    row_k = (r_of & (LAT_CH - 1)) * 4 + (r_of >> 5) * 2 + ((r_of >> 4) & 1)
    order = k_of == row_k
    final_rows = jnp.dot(order.astype(BF16), final_t[...], preferred_element_type=F32)
    rows_t[...] = final_rows.astype(BF16)
    gated = final_rows * gate[...]
    gated_hi = gated.astype(BF16)
    gated_lo = (gated - gated_hi.astype(F32)).astype(BF16)
    loads[2].wait()
    w2_f = lax.dot_general(
        jnp.concatenate([gated_hi, gated_lo], axis=0), weight_v[...], NT, preferred_element_type=F32
    )
    w2_f = w2_f[:vec] + w2_f[vec:]
    w2_hi = w2_f.astype(BF16)
    w2[:vec, :] = w2_hi
    w2[vec:, :] = (w2_f - w2_hi.astype(F32)).astype(BF16)
    middle(1)

    for h in range(heads):
        own_copies[h].wait()
        before(h)
        cols = slice(h * HEAD_DIM, (h + 1) * HEAD_DIM)

        @pl.loop(0, REFRESH, step=2)
        def _(base):
            pair = (base, base + 1)
            scores = [
                lax.dot_general(
                    keys[:, cols], q_all[h][refresh[s]], NT, preferred_element_type=F32
                )
                for s in pair
            ]
            nums = []
            for s, score in zip(pair, scores):
                top = jnp.max(score, axis=0, keepdims=True)
                weights = jnp.exp((score - top) * SCALE)
                stats[h][me, pl.ds(s, 1), :] = top
                stats[h][me, pl.ds(s + REFRESH, 1), :] = jnp.sum(weights, axis=0, keepdims=True)
                nums.append(
                    jnp.dot(values_t[h], weights.astype(BF16), preferred_element_type=F32)
                )
            for s, num in zip(pair, nums):
                num_hi = num.astype(BF16)
                num_lo = (num - num_hi.astype(F32)).astype(BF16)
                both = jnp.dot(w2[:, cols], num_hi, preferred_element_type=F32)
                rest = jnp.dot(w2[:vec, cols], num_lo, preferred_element_type=F32)
                u_buf[h, s] = both[:vec] + both[vec:] + rest

            pl.when(base == 0)(functools.partial(between, h))

        publish(h)
        refill(h)

    sums = [jnp.zeros((vec, tok), F32) for _ in range(REFRESH)]
    for h in range(heads):
        every = collect(h)
        tops, dens = every[:, :REFRESH], every[:, REFRESH:]
        top = jnp.max(tops, axis=0)
        den = jnp.sum(dens * jnp.exp((tops - top[None]) * SCALE), axis=0)
        factor = jnp.exp((stats[h][me][:REFRESH] - top) * SCALE) / den
        for s in range(REFRESH):
            sums[s] = sums[s] + u_buf[h, s] * factor[s : s + 1]
    for p in range(n):
        for s in range(REFRESH):
            rs_out[p, s] = sums[s][p * rows : (p + 1) * rows]

    def rs_copy(d):
        to = other(d)
        return remote(rs_out.at[to], rs_in.at[d], rs_send.at[d], rs_recv.at[d], patch=to)

    peers(n, lambda d: rs_copy(d).start())
    loads[3].wait()
    bias_col = jnp.sum(jnp.where(order, bias[...], 0.0), axis=1, keepdims=True)
    hid_t[...] = bias_col + lax.dot_general(
        rows_t[...], hidden_v[...], NT, preferred_element_type=F32
    )
    peers(n, lambda d: rs_copy(d).wait_recv())
    total = rs_out[me]
    for d in range(1, n):
        total = total + rs_in[d]
    z_out[...] = total

    def z_copy(d):
        to = other_z(d)
        return remote(z_out.at[to], z_in.at[d], z_send.at[d], z_recv.at[d], head=to)

    peers(nz, lambda d: z_copy(d).start())
    rr, cc = iota(spread.shape, 0), iota(spread.shape, 1)
    spread[...] = (cc == jnp.where(rr < tok, 2 * rr, 2 * (rr - tok) + 1)).astype(BF16)
    peers(nz, lambda d: z_copy(d).wait_recv())
    total = z_out[mz]
    for d in range(1, nz):
        total = total + z_in[d]
    z_all[mz] = total

    def zg_copy(d):
        part = z_all.at[mz]
        return remote(part, part, zg_send.at[d], zg_recv.at[d], head=other_z(d))

    peers(nz, lambda d: zg_copy(d).start())
    peers(nz, lambda d: zg_copy(d).wait_recv())
    for p in range(n):
        part = z_all[0]
        for s in range(1, REFRESH):
            part = jnp.where(refresh[s] == p, z_all[s], part)
        ag_out[p] = part

    def ag_copy(d):
        to = other(d)
        return remote(ag_out.at[to], ag.at[me], ag_send.at[d], ag_recv.at[d], patch=to)

    peers(n, lambda d: ag_copy(d).start())
    ag[me] = ag_out[me]
    peers(n, lambda d: ag_copy(d).wait_recv())
    parts = [ag[p] for p in range(n)]
    velocity = jnp.concatenate(parts, axis=0) + hid_t[...]
    wide = [
        jnp.concatenate([velocity[a * 32 : a * 32 + 16], velocity[a * 32 + 16 : a * 32 + 32]], axis=1)
        for a in range(2)
    ]
    wide = jnp.concatenate(wide, axis=0)
    one = wide.astype(BF16)
    left = wide - one.astype(F32)
    two = left.astype(BF16)
    three = (left - two.astype(F32)).astype(BF16)
    pieces = jnp.dot(
        jnp.concatenate([one, two, three], axis=0), spread[...], preferred_element_type=F32
    )
    field = pieces[:32] + pieces[32:64] + pieces[64:]
    for a in range(2):
        fresh_row = field[a * LAT_CH : (a + 1) * LAT_CH]
        row = jnp.where(mine, fresh_row, cache[a].astype(F32))
        latent = noisy[a].astype(F32) - noise[0] * row
        dec[a] = (latent / 0.3611 + 0.1159).astype(BF16)

    after, prior = lax.rem(me + 1, n), lax.rem(me + n - 1, n)
    edges = [
        remote(dec.at[1], halo.at[0], halo_send.at[0], halo_recv.at[0], patch=after),
        remote(dec.at[0], halo.at[1], halo_send.at[1], halo_recv.at[1], patch=prior),
    ]
    for copy in edges:
        copy.start()
    for copy in edges:
        copy.wait_recv()
    lines = [
        jnp.where(me > 0, halo[0].astype(F32), 0.0),
        dec[0].astype(F32),
        dec[1].astype(F32),
        jnp.where(me < n - 1, halo[1].astype(F32), 0.0),
    ]
    width = dec.shape[2]
    column = iota((LAT_CH, width), 1)
    shifted = []
    for line in lines:
        before_it = jnp.where(column == 0, 0.0, pltpu.roll(line, 1, 1))
        after_it = jnp.where(column == width - 1, 0.0, pltpu.roll(line, width - 1, 1))
        shifted.append([x.astype(BF16) for x in (before_it, line, after_it)])
    conv_col = to_column(conv_bias[...])
    for a in range(2):
        stencil = jnp.concatenate([shifted[a + u][v] for u in range(3) for v in range(3)], axis=0)
        result = lax.dot_general(conv_t[...], stencil, TN, preferred_element_type=F32)
        out[a] = (result + conv_col).astype(BF16)

    sent()
    for h in range(heads):
        published(h)
    peers(n, lambda d: rs_copy(d).wait_send())
    peers(nz, lambda d: z_copy(d).wait_send())
    peers(nz, lambda d: zg_copy(d).wait_send())
    peers(n, lambda d: ag_copy(d).wait_send())
    for copy in edges:
        copy.wait_send()


def on_device(
    n,
    nz,
    fresh_qkv,
    kv_cache,
    hidden,
    refresh,
    out_weight,
    final_weight,
    final_bias,
    gate_scale,
    noise_level,
    noisy_latent,
    velocity_cache,
    conv_weight,
    conv_bias,
):
    tok, _, local = fresh_qkv.shape
    heads = local // HEAD_DIM
    depth, vec = final_weight.shape
    rows = vec // n
    assert nz == REFRESH
    width = noisy_latent.shape[2]
    channels = conv_weight.shape[0]
    vmem, smem, anyw = (pl.BlockSpec(memory_space=m) for m in (pltpu.VMEM, pltpu.SMEM, pl.ANY))
    dma = pltpu.SemaphoreType.DMA
    kinds = 8 if n == 8 else n
    scratch = (
        [pltpu.VMEM((n, tok, HEAD_DIM), BF16)] * q_slots(n, heads)
        + [pltpu.VMEM((n, 2 * REFRESH, tok), F32)] * heads
        + [pltpu.VMEM((max(n // 2, 1), 2 * REFRESH, tok), F32)] * heads
        + [
            pltpu.VMEM((2, tok, local), BF16),
            pltpu.VMEM((tok, depth), BF16),
            pltpu.VMEM((local, depth), BF16),
            pltpu.VMEM((tok, local), BF16),
            pltpu.VMEM((heads, HEAD_DIM, tok), BF16),
            pltpu.VMEM((2 * vec, local), BF16),
            pltpu.VMEM((heads, REFRESH, vec, tok), F32),
            pltpu.VMEM((2 * tok, 2 * tok), BF16),
            pltpu.VMEM((vec, tok), F32),
            pltpu.VMEM((vec, depth), BF16),
            pltpu.VMEM((n, REFRESH, rows, tok), F32),
            pltpu.VMEM((n, REFRESH, rows, tok), F32),
            pltpu.VMEM((nz, rows, tok), F32),
            pltpu.VMEM((nz, rows, tok), F32),
            pltpu.VMEM((nz, rows, tok), F32),
            pltpu.VMEM((n, rows, tok), F32),
            pltpu.VMEM((n, rows, tok), F32),
            pltpu.VMEM((2, LAT_CH, width), BF16),
            pltpu.VMEM((2, LAT_CH, width), BF16),
            dma((4,)),
            dma((heads,)),
            dma((heads, kinds)),
            dma((heads, kinds)),
            dma((heads, n)),
            dma((heads, n)),
            dma((n,)),
            dma((n,)),
            dma((nz,)),
            dma((nz,)),
            dma((nz,)),
            dma((nz,)),
            dma((n,)),
            dma((n,)),
            dma((2,)),
            dma((2,)),
            pltpu.SemaphoreType.REGULAR((heads,)),
        ]
    )
    return pl.pallas_call(
        functools.partial(kernel, n, nz, heads, tok),
        out_shape=jax.ShapeDtypeStruct((2, channels, width), BF16),
        in_specs=[smem, smem, anyw, vmem, anyw, anyw] + [vmem] * 7,
        out_specs=vmem,
        scratch_shapes=scratch,
        compiler_params=pltpu.CompilerParams(
            collective_id=0, has_side_effects=True, vmem_limit_bytes=58 * 1024 * 1024
        ),
    )(
        refresh,
        noise_level,
        jnp.transpose(fresh_qkv, (1, 0, 2)),
        kv_cache,
        hidden,
        out_weight,
        final_weight.T,
        final_bias[None, :],
        gate_scale[None, :],
        noisy_latent,
        velocity_cache,
        jnp.transpose(conv_weight, (1, 2, 3, 0)).reshape(-1, channels),
        conv_bias[None, :],
    )


def solution(mesh):
    return jax.shard_map(
        functools.partial(on_device, mesh.shape["patch"], mesh.shape["head"]),
        mesh=mesh,
        in_specs=(
            P("patch", None, "head"),
            P("patch", None, "head"),
            P("patch", None),
            P(),
            P("head", None),
            P(),
            P(),
            P(),
            P(),
            P("patch", None, None),
            P("patch", None, None),
            P("head", None, None, None),
            P("head"),
        ),
        out_specs=P("patch", "head", None),
        check_vma=False,
    )
```

```python
import functools
import math

import jax
import jax.numpy as jnp
from jax import lax
from jax.experimental import pallas as pl
from jax.experimental.pallas import tpu as pltpu
from jax.sharding import PartitionSpec as P

HEAD_DIM = 128
LAT_CH = 16
REFRESH = 4
MESH = pl.DeviceIdType.MESH
SCALE = math.log2(math.e) / math.sqrt(HEAD_DIM)
NT = (((1,), (1,)), ((), ()))
TN = (((0,), (0,)), ((), ()))
F32 = jnp.float32
BF16 = jnp.bfloat16


def iota(shape, dim):
    return lax.broadcasted_iota(jnp.int32, shape, dim)


def q_slots(n, heads):
    return heads if n == 8 else min(2, heads)


def to_column(row):
    size = row.shape[1]
    eye = iota((size, size), 0) == iota((size, size), 1)
    return jnp.sum(jnp.where(eye, row, 0.0), axis=1, keepdims=True)


def kernel(
    n,
    nz,
    heads,
    tok,
    refresh,
    noise,
    fresh,
    kv,
    hidden,
    out_weight,
    final_t,
    bias,
    gate,
    noisy,
    cache,
    conv_t,
    conv_bias,
    out,
    *scratch,
):
    slots = q_slots(n, heads)
    q_all = [scratch[h % slots] for h in range(heads)]
    stats = scratch[slots : slots + heads]
    chips = scratch[slots + heads : slots + 2 * heads]
    (
        fresh_kv,
        hidden_v,
        weight_v,
        keys,
        values_t,
        w2,
        u_buf,
        spread,
        hid_t,
        rows_t,
        num_buf,
        rs_out,
        rs_in,
        z_out,
        z_in,
        z_all,
        ag_out,
        ag,
        dec,
        halo,
        load_sem,
        own_sem,
        q_send,
        q_recv,
        st_send,
        st_recv,
        rs_send,
        rs_recv,
        z_send,
        z_recv,
        zg_send,
        zg_recv,
        ag_send,
        ag_recv,
        halo_send,
        halo_recv,
        free_sem,
    ) = scratch[slots + 2 * heads :]
    me = lax.axis_index("patch")
    mz = lax.axis_index("head")
    vec = final_t.shape[0]
    rows = vec // n

    def peers(count, body):
        if count <= 8:
            for step in range(1, count):
                body(step)
        else:
            pl.loop(1, count)(body)

    def other(step):
        return lax.rem(me + step, n)

    def other_z(step):
        return lax.rem(mz + step, nz)

    def remote(src, dst, send, recv, **where):
        return pltpu.make_async_remote_copy(
            src_ref=src,
            dst_ref=dst,
            send_sem=send,
            recv_sem=recv,
            device_id=where,
            device_id_type=MESH,
        )

    loads = [
        pltpu.make_async_copy(fresh.at[1], fresh_kv.at[0], load_sem.at[0]),
        pltpu.make_async_copy(fresh.at[2], fresh_kv.at[1], load_sem.at[1]),
        pltpu.make_async_copy(out_weight, weight_v, load_sem.at[2]),
        pltpu.make_async_copy(hidden, hidden_v, load_sem.at[3]),
    ]
    own_q = [fresh.at[0, :, pl.ds(h * HEAD_DIM, HEAD_DIM)] for h in range(heads)]
    own_copies = [
        pltpu.make_async_copy(own_q[h], q_all[h].at[me], own_sem.at[h]) for h in range(heads)
    ]
    for copy in loads + own_copies[:slots]:
        copy.start()

    barrier = pltpu.get_barrier_semaphore()
    peers(n, lambda d: pl.semaphore_signal(
        barrier, inc=1, device_id={"patch": other(d)}, device_id_type=MESH))
    peers(nz, lambda d: pl.semaphore_signal(
        barrier, inc=1, device_id={"head": other_z(d)}, device_id_type=MESH))
    pl.semaphore_wait(barrier, n - 1 + nz - 1)

    def st_copy(h, d):
        part = stats[h].at[me]
        return remote(part, part, st_send.at[h, d], st_recv.at[h, d], patch=other(d))

    if n == 8:
        near = me + 1 - 2 * lax.rem(me, 2)
        side = me + 2 - 4 * lax.rem(me // 2, 2)
        over = me + 4 - 8 * (me // 4)
        diag = side + over - me
        half = tok // 2
        low, high = pl.ds(0, half), pl.ds(half, half)
        near_of = lambda p: p + near - me

        def q_copy(h, kind, src, dst, to):
            return remote(src, dst, q_send.at[h, kind], q_recv.at[h, kind], patch=to)

        def first(h):
            dst = q_all[h].at[me]
            return [q_copy(h, k, own_q[h], dst, to) for k, to in ((0, side), (1, over), (2, near))]

        def second(h):
            from_side, from_over = q_all[h].at[side], q_all[h].at[over]
            return [
                q_copy(h, 3, from_side.at[low], from_side.at[low], over),
                q_copy(h, 4, from_over.at[high], from_over.at[high], side),
                q_copy(h, 5, from_side, from_side, near),
                q_copy(h, 6, from_over, from_over, near),
            ]

        def third(h):
            block = q_all[h].at[diag]
            return [q_copy(h, 7, block, block, near)]

        def arrive(h, kind, dst):
            q_copy(h, kind, dst, dst, near).wait_recv()

        def start(copies):
            for copy in copies:
                copy.start()

        def relay(h):
            arrive(h, 0, q_all[h].at[side])
            arrive(h, 1, q_all[h].at[over])
            start(second(h))

        def relay_last(h):
            arrive(h, 3, q_all[h].at[diag].at[low])
            arrive(h, 4, q_all[h].at[diag].at[high])
            start(third(h))

        def before(h):
            arrive(h, 2, q_all[h].at[near])
            arrive(h, 5, q_all[h].at[near_of(side)])
            arrive(h, 6, q_all[h].at[near_of(over)])
            arrive(h, 7, q_all[h].at[near_of(diag)])

        def between(h):
            if h + 1 < heads:
                relay_last(h + 1)
            if h + 2 < heads:
                relay(h + 2)
            if h + 5 < heads:
                start(first(h + 5))
            if h >= 1:
                chip_stats(h - 1)

        def chip_copies(h):
            part = chips[h].at[me // 2]
            return [
                remote(part, part, st_send.at[h, k], st_recv.at[h, k], patch=to)
                for k, to in ((1, side), (2, over), (3, diag))
            ]

        def chip_stats(h):
            near_copy(h).wait_recv()
            both = (stats[h][me], stats[h][near])
            tops = [x[:REFRESH] for x in both]
            top = jnp.maximum(*tops)
            den = sum(x[REFRESH:] * jnp.exp2((x[:REFRESH] - top) * SCALE) for x in both)
            chips[h][me // 2, :REFRESH] = top
            chips[h][me // 2, REFRESH:] = den
            start(chip_copies(h))

        def near_copy(h):
            part = stats[h].at[me]
            return remote(part, part, st_send.at[h, 0], st_recv.at[h, 0], patch=near)

        def publish(h):
            if h < heads - 1:
                near_copy(h).start()
            else:
                peers(n, lambda d: st_copy(h, d).start())

        def collect(h):
            if h < heads - 1:
                for copy in chip_copies(h):
                    copy.wait_recv()
                return chips[h][...]
            peers(n, lambda d: st_copy(h, d).wait_recv())
            return stats[h][...]

        def published(h):
            if h < heads - 1:
                near_copy(h).wait_send()
                for copy in chip_copies(h):
                    copy.wait_send()
            else:
                peers(n, lambda d: st_copy(h, d).wait_send())

        def prologue():
            for h in range(min(3, heads)):
                start(first(h))

        def middle(part):
            if part == 0:
                relay(0)
                if heads > 3:
                    start(first(3))
            else:
                relay_last(0)
                if heads > 1:
                    relay(1)
                if heads > 4:
                    start(first(4))

        def refill(h):
            pass

        def sent():
            for h in range(heads):
                for copy in first(h) + second(h) + third(h):
                    copy.wait_send()

    else:

        def direct(h, d):
            return remote(
                own_q[h], q_all[h].at[me], q_send.at[h, d], q_recv.at[h, d], patch=other(d)
            )

        def prologue():
            for h in range(slots):
                peers(n, lambda d: direct(h, d).start())

        def refill(h):
            later = h + slots
            if later < heads:
                peers(n, lambda d: pl.semaphore_signal(
                    free_sem.at[h], inc=1, device_id={"patch": other(d)}, device_id_type=MESH))
                pl.semaphore_wait(free_sem.at[h], n - 1)
                own_copies[later].start()
                peers(n, lambda d: direct(later, d).start())

        def middle(part):
            pass

        def between(h):
            pass

        def publish(h):
            peers(n, lambda d: st_copy(h, d).start())

        def collect(h):
            peers(n, lambda d: st_copy(h, d).wait_recv())
            return stats[h][...]

        def published(h):
            peers(n, lambda d: st_copy(h, d).wait_send())

        def before(h):
            peers(n, lambda d: direct(h, d).wait_recv())

        def sent():
            for h in range(heads):
                peers(n, lambda d: direct(h, d).wait_send())

    prologue()

    is_mine = [refresh[s] == me for s in range(REFRESH)]
    mine = is_mine[0] | is_mine[1] | is_mine[2] | is_mine[3]
    group = 128
    r, c = iota((2 * group, 2 * group), 0), iota((2 * group, 2 * group), 1)
    unmix = (c == jnp.where(r < group, 2 * r, 2 * (r - group) + 1)).astype(BF16)
    eye = (iota((HEAD_DIM, HEAD_DIM), 0) == iota((HEAD_DIM, HEAD_DIM), 1)).astype(BF16)
    loads[0].wait()
    loads[1].wait()
    for g in range(tok // group):
        at = pl.ds(g * group, group)
        mixed = jnp.dot(unmix, kv[pl.ds(g * group, group)].reshape(2 * group, -1), preferred_element_type=F32)
        mixed = mixed.astype(BF16)
        keys[at, :] = jnp.where(mine, fresh_kv[0, at, :], mixed[:group])
        picked = jnp.where(mine, fresh_kv[1, at, :], mixed[group:])
        for h in range(heads):
            cols = slice(h * HEAD_DIM, (h + 1) * HEAD_DIM)
            values_t[h, :, at] = lax.dot_general(
                eye, picked[:, cols], NT, preferred_element_type=F32
            ).astype(BF16)
    middle(0)

    middle(1)

    for h in range(heads):
        own_copies[h].wait()
        before(h)
        cols = slice(h * HEAD_DIM, (h + 1) * HEAD_DIM)

        @pl.loop(0, REFRESH, step=2)
        def _(base):
            pair = (base, base + 1)
            scores = [
                lax.dot_general(
                    keys[:, cols], q_all[h][refresh[s]], NT, preferred_element_type=F32
                )
                for s in pair
            ]
            nums = []
            for s, score in zip(pair, scores):
                top = jnp.max(score, axis=0, keepdims=True)
                weights = jnp.exp2((score - top) * SCALE)
                stats[h][me, pl.ds(s, 1), :] = top
                stats[h][me, pl.ds(s + REFRESH, 1), :] = jnp.sum(weights, axis=0, keepdims=True)
                nums.append(
                    jnp.dot(values_t[h], weights.astype(BF16), preferred_element_type=F32)
                )
            for s, num in zip(pair, nums):
                num_buf[s] = num

            pl.when(base == 0)(functools.partial(between, h))

        publish(h)
        refill(h)
        if h == 0:
            k_of = iota((vec, vec), 1)
            r_of = iota((vec, vec), 0)
            row_k = (r_of & (LAT_CH - 1)) * 4 + (r_of >> 5) * 2 + ((r_of >> 4) & 1)
            order = k_of == row_k
            final_rows = jnp.dot(order.astype(BF16), final_t[...], preferred_element_type=F32)
            rows_t[...] = final_rows.astype(BF16)
            gated = final_rows * gate[...]
            gated_hi = gated.astype(BF16)
            gated_lo = (gated - gated_hi.astype(F32)).astype(BF16)
            loads[2].wait()
            w2_f = lax.dot_general(
                jnp.concatenate([gated_hi, gated_lo], axis=0), weight_v[...], NT, preferred_element_type=F32
            )
            w2_f = w2_f[:vec] + w2_f[vec:]
            w2_hi = w2_f.astype(BF16)
            w2[:vec, :] = w2_hi
            w2[vec:, :] = (w2_f - w2_hi.astype(F32)).astype(BF16)

        @pl.loop(0, REFRESH)
        def _(s):
            num = num_buf[s]
            num_hi = num.astype(BF16)
            num_lo = (num - num_hi.astype(F32)).astype(BF16)
            both = jnp.dot(w2[:, cols], num_hi, preferred_element_type=F32)
            rest = jnp.dot(w2[:vec, cols], num_lo, preferred_element_type=F32)
            u_buf[h, s] = both[:vec] + both[vec:] + rest

    sums = [jnp.zeros((vec, tok), F32) for _ in range(REFRESH)]
    for h in range(heads):
        every = collect(h)
        tops, dens = every[:, :REFRESH], every[:, REFRESH:]
        top = jnp.max(tops, axis=0)
        den = jnp.sum(dens * jnp.exp2((tops - top[None]) * SCALE), axis=0)
        factor = jnp.exp2((stats[h][me][:REFRESH] - top) * SCALE) / den
        for s in range(REFRESH):
            sums[s] = sums[s] + u_buf[h, s] * factor[s : s + 1]
    for p in range(n):
        for s in range(REFRESH):
            part = sums[s][p * rows : (p + 1) * rows]
            rs_out[p, s * rows : (s + 1) * rows] = part.astype(rs_out.dtype)

    def rs_copy(d):
        to = other(d)
        return remote(rs_out.at[to], rs_in.at[d], rs_send.at[d], rs_recv.at[d], patch=to)

    peers(n, lambda d: rs_copy(d).start())
    loads[3].wait()
    bias_col = jnp.sum(jnp.where(order, bias[...], 0.0), axis=1, keepdims=True)
    hid_t[...] = bias_col + lax.dot_general(
        rows_t[...], hidden_v[...], NT, preferred_element_type=F32
    )
    peers(n, lambda d: rs_copy(d).wait_recv())
    total = rs_out[me].astype(F32)
    for d in range(1, n):
        total = total + rs_in[d].astype(F32)
    for s in range(REFRESH):
        z_out[s] = total[s * rows : (s + 1) * rows]

    def z_copy(d):
        to = other_z(d)
        return remote(z_out.at[to], z_in.at[d], z_send.at[d], z_recv.at[d], head=to)

    peers(nz, lambda d: z_copy(d).start())
    rr, cc = iota(spread.shape, 0), iota(spread.shape, 1)
    spread[...] = (cc == jnp.where(rr < tok, 2 * rr, 2 * (rr - tok) + 1)).astype(BF16)
    peers(nz, lambda d: z_copy(d).wait_recv())
    total = z_out[mz]
    for d in range(1, nz):
        total = total + z_in[d]
    z_all[mz] = total

    def zg_copy(d):
        part = z_all.at[mz]
        return remote(part, part, zg_send.at[d], zg_recv.at[d], head=other_z(d))

    peers(nz, lambda d: zg_copy(d).start())
    peers(nz, lambda d: zg_copy(d).wait_recv())
    for p in range(n):
        part = z_all[0]
        for s in range(1, REFRESH):
            part = jnp.where(refresh[s] == p, z_all[s], part)
        ag_out[p] = part

    def ag_copy(d):
        to = other(d)
        return remote(ag_out.at[to], ag.at[me], ag_send.at[d], ag_recv.at[d], patch=to)

    peers(n, lambda d: ag_copy(d).start())
    ag[me] = ag_out[me]
    peers(n, lambda d: ag_copy(d).wait_recv())
    parts = [ag[p] for p in range(n)]
    velocity = jnp.concatenate(parts, axis=0) + hid_t[...]
    wide = [
        jnp.concatenate([velocity[a * 32 : a * 32 + 16], velocity[a * 32 + 16 : a * 32 + 32]], axis=1)
        for a in range(2)
    ]
    wide = jnp.concatenate(wide, axis=0)
    one = wide.astype(BF16)
    left = wide - one.astype(F32)
    two = left.astype(BF16)
    three = (left - two.astype(F32)).astype(BF16)
    pieces = jnp.dot(
        jnp.concatenate([one, two, three], axis=0), spread[...], preferred_element_type=F32
    )
    field = pieces[:32] + pieces[32:64] + pieces[64:]
    for a in range(2):
        fresh_row = field[a * LAT_CH : (a + 1) * LAT_CH]
        row = jnp.where(mine, fresh_row, cache[a].astype(F32))
        latent = noisy[a].astype(F32) - noise[0] * row
        dec[a] = (latent / 0.3611 + 0.1159).astype(BF16)

    after, prior = lax.rem(me + 1, n), lax.rem(me + n - 1, n)
    edges = [
        remote(dec.at[1], halo.at[0], halo_send.at[0], halo_recv.at[0], patch=after),
        remote(dec.at[0], halo.at[1], halo_send.at[1], halo_recv.at[1], patch=prior),
    ]
    for copy in edges:
        copy.start()
    for copy in edges:
        copy.wait_recv()
    lines = [
        jnp.where(me > 0, halo[0].astype(F32), 0.0),
        dec[0].astype(F32),
        dec[1].astype(F32),
        jnp.where(me < n - 1, halo[1].astype(F32), 0.0),
    ]
    width = dec.shape[2]
    column = iota((LAT_CH, width), 1)
    shifted = []
    for line in lines:
        before_it = jnp.where(column == 0, 0.0, pltpu.roll(line, 1, 1))
        after_it = jnp.where(column == width - 1, 0.0, pltpu.roll(line, width - 1, 1))
        shifted.append([x.astype(BF16) for x in (before_it, line, after_it)])
    conv_col = to_column(conv_bias[...])
    for a in range(2):
        stencil = jnp.concatenate([shifted[a + u][v] for u in range(3) for v in range(3)], axis=0)
        result = lax.dot_general(conv_t[...], stencil, TN, preferred_element_type=F32)
        out[a] = (result + conv_col).astype(BF16)

    sent()
    for h in range(heads):
        published(h)
    peers(n, lambda d: rs_copy(d).wait_send())
    peers(nz, lambda d: z_copy(d).wait_send())
    peers(nz, lambda d: zg_copy(d).wait_send())
    peers(n, lambda d: ag_copy(d).wait_send())
    for copy in edges:
        copy.wait_send()


def on_device(
    n,
    nz,
    fresh_qkv,
    kv_cache,
    hidden,
    refresh,
    out_weight,
    final_weight,
    final_bias,
    gate_scale,
    noise_level,
    noisy_latent,
    velocity_cache,
    conv_weight,
    conv_bias,
):
    tok, _, local = fresh_qkv.shape
    heads = local // HEAD_DIM
    depth, vec = final_weight.shape
    rows = vec // n
    assert nz == REFRESH
    width = noisy_latent.shape[2]
    channels = conv_weight.shape[0]
    vmem, smem, anyw = (pl.BlockSpec(memory_space=m) for m in (pltpu.VMEM, pltpu.SMEM, pl.ANY))
    dma = pltpu.SemaphoreType.DMA
    kinds = 8 if n == 8 else n
    scratch = (
        [pltpu.VMEM((n, tok, HEAD_DIM), BF16)] * q_slots(n, heads)
        + [pltpu.VMEM((n, 2 * REFRESH, tok), F32)] * heads
        + [pltpu.VMEM((max(n // 2, 1), 2 * REFRESH, tok), F32)] * heads
        + [
            pltpu.VMEM((2, tok, local), BF16),
            pltpu.VMEM((tok, depth), BF16),
            pltpu.VMEM((local, depth), BF16),
            pltpu.VMEM((tok, local), BF16),
            pltpu.VMEM((heads, HEAD_DIM, tok), BF16),
            pltpu.VMEM((2 * vec, local), BF16),
            pltpu.VMEM((heads, REFRESH, vec, tok), F32),
            pltpu.VMEM((2 * tok, 2 * tok), BF16),
            pltpu.VMEM((vec, tok), F32),
            pltpu.VMEM((vec, depth), BF16),
            pltpu.VMEM((REFRESH, HEAD_DIM, tok), F32),
            pltpu.VMEM((n, REFRESH * rows, tok), BF16 if rows % 8 == 0 else F32),
            pltpu.VMEM((n, REFRESH * rows, tok), BF16 if rows % 8 == 0 else F32),
            pltpu.VMEM((nz, rows, tok), F32),
            pltpu.VMEM((nz, rows, tok), F32),
            pltpu.VMEM((nz, rows, tok), F32),
            pltpu.VMEM((n, rows, tok), F32),
            pltpu.VMEM((n, rows, tok), F32),
            pltpu.VMEM((2, LAT_CH, width), BF16),
            pltpu.VMEM((2, LAT_CH, width), BF16),
            dma((4,)),
            dma((heads,)),
            dma((heads, kinds)),
            dma((heads, kinds)),
            dma((heads, n)),
            dma((heads, n)),
            dma((n,)),
            dma((n,)),
            dma((nz,)),
            dma((nz,)),
            dma((nz,)),
            dma((nz,)),
            dma((n,)),
            dma((n,)),
            dma((2,)),
            dma((2,)),
            pltpu.SemaphoreType.REGULAR((heads,)),
        ]
    )
    return pl.pallas_call(
        functools.partial(kernel, n, nz, heads, tok),
        out_shape=jax.ShapeDtypeStruct((2, channels, width), BF16),
        in_specs=[smem, smem, anyw, vmem, anyw, anyw] + [vmem] * 7,
        out_specs=vmem,
        scratch_shapes=scratch,
        compiler_params=pltpu.CompilerParams(
            collective_id=0, has_side_effects=True, vmem_limit_bytes=58 * 1024 * 1024
        ),
    )(
        refresh,
        noise_level,
        jnp.transpose(fresh_qkv, (1, 0, 2)),
        kv_cache,
        hidden,
        out_weight,
        final_weight.T,
        final_bias[None, :],
        gate_scale[None, :],
        noisy_latent,
        velocity_cache,
        jnp.transpose(conv_weight, (1, 2, 3, 0)).reshape(-1, channels),
        conv_bias[None, :],
    )


def solution(mesh):
    return jax.shard_map(
        functools.partial(on_device, mesh.shape["patch"], mesh.shape["head"]),
        mesh=mesh,
        in_specs=(
            P("patch", None, "head"),
            P("patch", None, "head"),
            P("patch", None),
            P(),
            P("head", None),
            P(),
            P(),
            P(),
            P(),
            P("patch", None, None),
            P("patch", None, None),
            P("head", None, None, None),
            P("head"),
        ),
        out_specs=P("patch", "head", None),
        check_vma=False,
    )
```

```python
import functools
import math

import jax
import jax.numpy as jnp
from jax import lax
from jax.experimental import pallas as pl
from jax.experimental.pallas import tpu as pltpu
from jax.sharding import PartitionSpec as P

HEAD_DIM = 128
LAT_CH = 16
REFRESH = 4
MESH = pl.DeviceIdType.MESH
SCALE = math.log2(math.e) / math.sqrt(HEAD_DIM)
NT = (((1,), (1,)), ((), ()))
TN = (((0,), (0,)), ((), ()))
F32 = jnp.float32
BF16 = jnp.bfloat16


def iota(shape, dim):
    return lax.broadcasted_iota(jnp.int32, shape, dim)


def q_slots(n, heads):
    return heads if n == 8 else min(2, heads)


def to_column(row):
    size = row.shape[1]
    eye = iota((size, size), 0) == iota((size, size), 1)
    return jnp.sum(jnp.where(eye, row, 0.0), axis=1, keepdims=True)


def kernel(
    n,
    nz,
    heads,
    tok,
    refresh,
    noise,
    fresh,
    kv,
    hidden,
    out_weight,
    final_t,
    bias,
    gate,
    noisy,
    cache,
    conv_t,
    conv_bias,
    out,
    *scratch,
):
    slots = q_slots(n, heads)
    q_all = [scratch[h % slots] for h in range(heads)]
    stats = scratch[slots : slots + heads]
    chips = scratch[slots + heads : slots + 2 * heads]
    (
        fresh_kv,
        hidden_v,
        weight_v,
        keys,
        values_t,
        w2,
        u_buf,
        spread,
        hid_t,
        rows_t,
        num_buf,
        rs_out,
        rs_in,
        z_out,
        z_in,
        z_all,
        ag_out,
        ag,
        dec,
        halo,
        load_sem,
        own_sem,
        q_send,
        q_recv,
        st_send,
        st_recv,
        rs_send,
        rs_recv,
        z_send,
        z_recv,
        zg_send,
        zg_recv,
        ag_send,
        ag_recv,
        halo_send,
        halo_recv,
        free_sem,
    ) = scratch[slots + 2 * heads :]
    me = lax.axis_index("patch")
    mz = lax.axis_index("head")
    vec = final_t.shape[0]
    rows = vec // n

    def peers(count, body):
        if count <= 8:
            for step in range(1, count):
                body(step)
        else:
            pl.loop(1, count)(body)

    def other(step):
        return lax.rem(me + step, n)

    def other_z(step):
        return lax.rem(mz + step, nz)

    def remote(src, dst, send, recv, **where):
        return pltpu.make_async_remote_copy(
            src_ref=src,
            dst_ref=dst,
            send_sem=send,
            recv_sem=recv,
            device_id=where,
            device_id_type=MESH,
        )

    loads = [
        pltpu.make_async_copy(fresh.at[1], fresh_kv.at[0], load_sem.at[0]),
        pltpu.make_async_copy(fresh.at[2], fresh_kv.at[1], load_sem.at[1]),
        pltpu.make_async_copy(out_weight, weight_v, load_sem.at[2]),
        pltpu.make_async_copy(hidden, hidden_v, load_sem.at[3]),
    ]
    own_q = [fresh.at[0, :, pl.ds(h * HEAD_DIM, HEAD_DIM)] for h in range(heads)]
    own_copies = [
        pltpu.make_async_copy(own_q[h], q_all[h].at[me], own_sem.at[h]) for h in range(heads)
    ]
    for copy in loads[:2] + own_copies[:slots]:
        copy.start()

    barrier = pltpu.get_barrier_semaphore()
    peers(n, lambda d: pl.semaphore_signal(
        barrier, inc=1, device_id={"patch": other(d)}, device_id_type=MESH))
    peers(nz, lambda d: pl.semaphore_signal(
        barrier, inc=1, device_id={"head": other_z(d)}, device_id_type=MESH))
    pl.semaphore_wait(barrier, n - 1 + nz - 1)

    def st_copy(h, d):
        part = stats[h].at[me]
        return remote(part, part, st_send.at[h, d], st_recv.at[h, d], patch=other(d))

    if n == 8:
        near = me + 1 - 2 * lax.rem(me, 2)
        side = me + 2 - 4 * lax.rem(me // 2, 2)
        over = me + 4 - 8 * (me // 4)
        diag = side + over - me
        half = tok // 2
        low, high = pl.ds(0, half), pl.ds(half, half)
        near_of = lambda p: p + near - me

        def q_copy(h, kind, src, dst, to):
            return remote(src, dst, q_send.at[h, kind], q_recv.at[h, kind], patch=to)

        def first(h):
            dst = q_all[h].at[me]
            return [q_copy(h, k, own_q[h], dst, to) for k, to in ((0, side), (1, over), (2, near))]

        def second(h):
            from_side, from_over = q_all[h].at[side], q_all[h].at[over]
            return [
                q_copy(h, 3, from_side.at[low], from_side.at[low], over),
                q_copy(h, 4, from_over.at[high], from_over.at[high], side),
                q_copy(h, 5, from_side, from_side, near),
                q_copy(h, 6, from_over, from_over, near),
            ]

        def third(h):
            block = q_all[h].at[diag]
            return [q_copy(h, 7, block, block, near)]

        def arrive(h, kind, dst):
            q_copy(h, kind, dst, dst, near).wait_recv()

        def start(copies):
            for copy in copies:
                copy.start()

        def relay(h):
            arrive(h, 0, q_all[h].at[side])
            arrive(h, 1, q_all[h].at[over])
            start(second(h))

        def relay_last(h):
            arrive(h, 3, q_all[h].at[diag].at[low])
            arrive(h, 4, q_all[h].at[diag].at[high])
            start(third(h))

        def before(h):
            arrive(h, 2, q_all[h].at[near])
            arrive(h, 5, q_all[h].at[near_of(side)])
            arrive(h, 6, q_all[h].at[near_of(over)])
            arrive(h, 7, q_all[h].at[near_of(diag)])

        def between(h):
            if h + 1 < heads:
                relay_last(h + 1)
            if h + 2 < heads:
                relay(h + 2)
            if h + 5 < heads:
                start(first(h + 5))
            if h >= 1:
                chip_stats(h - 1)

        def chip_copies(h):
            part = chips[h].at[me // 2]
            return [
                remote(part, part, st_send.at[h, k], st_recv.at[h, k], patch=to)
                for k, to in ((1, side), (2, over), (3, diag))
            ]

        def chip_stats(h):
            near_copy(h).wait_recv()
            both = (stats[h][me], stats[h][near])
            tops = [x[:REFRESH] for x in both]
            top = jnp.maximum(*tops)
            den = sum(x[REFRESH:] * jnp.exp2((x[:REFRESH] - top) * SCALE) for x in both)
            chips[h][me // 2, :REFRESH] = top
            chips[h][me // 2, REFRESH:] = den
            start(chip_copies(h))

        def near_copy(h):
            part = stats[h].at[me]
            return remote(part, part, st_send.at[h, 0], st_recv.at[h, 0], patch=near)

        def publish(h):
            if h < heads - 1:
                near_copy(h).start()
            else:
                peers(n, lambda d: st_copy(h, d).start())

        def collect(h):
            if h < heads - 1:
                for copy in chip_copies(h):
                    copy.wait_recv()
                return chips[h][...]
            peers(n, lambda d: st_copy(h, d).wait_recv())
            return stats[h][...]

        def published(h):
            if h < heads - 1:
                near_copy(h).wait_send()
                for copy in chip_copies(h):
                    copy.wait_send()
            else:
                peers(n, lambda d: st_copy(h, d).wait_send())

        def prologue():
            for h in range(min(3, heads)):
                start(first(h))

        def middle(part):
            if part == 0:
                relay(0)
                if heads > 3:
                    start(first(3))
            else:
                relay_last(0)
                if heads > 1:
                    relay(1)
                if heads > 4:
                    start(first(4))

        def refill(h):
            pass

        def sent():
            for h in range(heads):
                for copy in first(h) + second(h) + third(h):
                    copy.wait_send()

    else:

        def direct(h, d):
            return remote(
                own_q[h], q_all[h].at[me], q_send.at[h, d], q_recv.at[h, d], patch=other(d)
            )

        def prologue():
            for h in range(slots):
                peers(n, lambda d: direct(h, d).start())

        def refill(h):
            later = h + slots
            if later < heads:
                peers(n, lambda d: pl.semaphore_signal(
                    free_sem.at[h], inc=1, device_id={"patch": other(d)}, device_id_type=MESH))
                pl.semaphore_wait(free_sem.at[h], n - 1)
                own_copies[later].start()
                peers(n, lambda d: direct(later, d).start())

        def middle(part):
            pass

        def between(h):
            pass

        def publish(h):
            peers(n, lambda d: st_copy(h, d).start())

        def collect(h):
            peers(n, lambda d: st_copy(h, d).wait_recv())
            return stats[h][...]

        def published(h):
            peers(n, lambda d: st_copy(h, d).wait_send())

        def before(h):
            peers(n, lambda d: direct(h, d).wait_recv())

        def sent():
            for h in range(heads):
                peers(n, lambda d: direct(h, d).wait_send())

    prologue()
    for copy in loads[2:]:
        copy.start()

    is_mine = [refresh[s] == me for s in range(REFRESH)]
    mine = is_mine[0] | is_mine[1] | is_mine[2] | is_mine[3]
    group = 128
    r, c = iota((2 * group, 2 * group), 0), iota((2 * group, 2 * group), 1)
    unmix = (c == jnp.where(r < group, 2 * r, 2 * (r - group) + 1)).astype(BF16)
    eye = (iota((HEAD_DIM, HEAD_DIM), 0) == iota((HEAD_DIM, HEAD_DIM), 1)).astype(BF16)
    loads[0].wait()
    loads[1].wait()
    for g in range(tok // group):
        at = pl.ds(g * group, group)
        mixed = jnp.dot(unmix, kv[pl.ds(g * group, group)].reshape(2 * group, -1), preferred_element_type=F32)
        mixed = mixed.astype(BF16)
        keys[at, :] = jnp.where(mine, fresh_kv[0, at, :], mixed[:group])
        picked = jnp.where(mine, fresh_kv[1, at, :], mixed[group:])
        for h in range(heads):
            cols = slice(h * HEAD_DIM, (h + 1) * HEAD_DIM)
            values_t[h, :, at] = lax.dot_general(
                eye, picked[:, cols], NT, preferred_element_type=F32
            ).astype(BF16)
    middle(0)

    middle(1)

    for h in range(heads):
        own_copies[h].wait()
        before(h)
        cols = slice(h * HEAD_DIM, (h + 1) * HEAD_DIM)

        @pl.loop(0, REFRESH, step=2)
        def _(base):
            pair = (base, base + 1)
            scores = [
                lax.dot_general(
                    keys[:, cols], q_all[h][refresh[s]], NT, preferred_element_type=F32
                )
                for s in pair
            ]
            nums = []
            for s, score in zip(pair, scores):
                top = jnp.max(score, axis=0, keepdims=True)
                weights = jnp.exp2((score - top) * SCALE)
                stats[h][me, pl.ds(s, 1), :] = top
                stats[h][me, pl.ds(s + REFRESH, 1), :] = jnp.sum(weights, axis=0, keepdims=True)
                nums.append(
                    jnp.dot(values_t[h], weights.astype(BF16), preferred_element_type=F32)
                )
            for s, num in zip(pair, nums):
                num_buf[s] = num

            pl.when(base == 0)(functools.partial(between, h))

        publish(h)
        refill(h)
        if h == 0:
            k_of = iota((vec, vec), 1)
            r_of = iota((vec, vec), 0)
            row_k = (r_of & (LAT_CH - 1)) * 4 + (r_of >> 5) * 2 + ((r_of >> 4) & 1)
            order = k_of == row_k
            final_rows = jnp.dot(order.astype(BF16), final_t[...], preferred_element_type=F32)
            rows_t[...] = final_rows.astype(BF16)
            gated = final_rows * gate[...]
            gated_hi = gated.astype(BF16)
            gated_lo = (gated - gated_hi.astype(F32)).astype(BF16)
            loads[2].wait()
            w2_f = lax.dot_general(
                jnp.concatenate([gated_hi, gated_lo], axis=0), weight_v[...], NT, preferred_element_type=F32
            )
            w2_f = w2_f[:vec] + w2_f[vec:]
            w2_hi = w2_f.astype(BF16)
            w2[:vec, :] = w2_hi
            w2[vec:, :] = (w2_f - w2_hi.astype(F32)).astype(BF16)

        @pl.loop(0, REFRESH)
        def _(s):
            num = num_buf[s]
            num_hi = num.astype(BF16)
            num_lo = (num - num_hi.astype(F32)).astype(BF16)
            both = jnp.dot(w2[:, cols], num_hi, preferred_element_type=F32)
            rest = jnp.dot(w2[:vec, cols], num_lo, preferred_element_type=F32)
            u_buf[h, s] = both[:vec] + both[vec:] + rest

    sums = [jnp.zeros((vec, tok), F32) for _ in range(REFRESH)]
    for h in range(heads):
        every = collect(h)
        tops, dens = every[:, :REFRESH], every[:, REFRESH:]
        top = jnp.max(tops, axis=0)
        den = jnp.sum(dens * jnp.exp2((tops - top[None]) * SCALE), axis=0)
        factor = jnp.exp2((stats[h][me][:REFRESH] - top) * SCALE) / den
        for s in range(REFRESH):
            sums[s] = sums[s] + u_buf[h, s] * factor[s : s + 1]
    for p in range(n):
        for s in range(REFRESH):
            part = sums[s][p * rows : (p + 1) * rows]
            rs_out[p, s * rows : (s + 1) * rows] = part.astype(rs_out.dtype)

    def rs_copy(d):
        to = other(d)
        return remote(rs_out.at[to], rs_in.at[d], rs_send.at[d], rs_recv.at[d], patch=to)

    peers(n, lambda d: rs_copy(d).start())
    loads[3].wait()
    bias_col = jnp.sum(jnp.where(order, bias[...], 0.0), axis=1, keepdims=True)
    hid_t[...] = bias_col + lax.dot_general(
        rows_t[...], hidden_v[...], NT, preferred_element_type=F32
    )
    peers(n, lambda d: rs_copy(d).wait_recv())
    total = rs_out[me].astype(F32)
    for d in range(1, n):
        total = total + rs_in[d].astype(F32)
    for s in range(REFRESH):
        z_out[s] = total[s * rows : (s + 1) * rows]

    def z_copy(d):
        to = other_z(d)
        return remote(z_out.at[to], z_in.at[d], z_send.at[d], z_recv.at[d], head=to)

    peers(nz, lambda d: z_copy(d).start())
    rr, cc = iota(spread.shape, 0), iota(spread.shape, 1)
    spread[...] = (cc == jnp.where(rr < tok, 2 * rr, 2 * (rr - tok) + 1)).astype(BF16)
    peers(nz, lambda d: z_copy(d).wait_recv())
    total = z_out[mz]
    for d in range(1, nz):
        total = total + z_in[d]
    z_all[mz] = total

    def zg_copy(d):
        part = z_all.at[mz]
        return remote(part, part, zg_send.at[d], zg_recv.at[d], head=other_z(d))

    peers(nz, lambda d: zg_copy(d).start())
    peers(nz, lambda d: zg_copy(d).wait_recv())
    for p in range(n):
        part = z_all[0]
        for s in range(1, REFRESH):
            part = jnp.where(refresh[s] == p, z_all[s], part)
        ag_out[p] = part

    def ag_copy(d):
        to = other(d)
        return remote(ag_out.at[to], ag.at[me], ag_send.at[d], ag_recv.at[d], patch=to)

    peers(n, lambda d: ag_copy(d).start())
    ag[me] = ag_out[me]
    peers(n, lambda d: ag_copy(d).wait_recv())
    parts = [ag[p] for p in range(n)]
    velocity = jnp.concatenate(parts, axis=0) + hid_t[...]
    wide = [
        jnp.concatenate([velocity[a * 32 : a * 32 + 16], velocity[a * 32 + 16 : a * 32 + 32]], axis=1)
        for a in range(2)
    ]
    wide = jnp.concatenate(wide, axis=0)
    one = wide.astype(BF16)
    left = wide - one.astype(F32)
    two = left.astype(BF16)
    three = (left - two.astype(F32)).astype(BF16)
    pieces = jnp.dot(
        jnp.concatenate([one, two, three], axis=0), spread[...], preferred_element_type=F32
    )
    field = pieces[:32] + pieces[32:64] + pieces[64:]
    for a in range(2):
        fresh_row = field[a * LAT_CH : (a + 1) * LAT_CH]
        row = jnp.where(mine, fresh_row, cache[a].astype(F32))
        latent = noisy[a].astype(F32) - noise[0] * row
        dec[a] = (latent / 0.3611 + 0.1159).astype(BF16)

    after, prior = lax.rem(me + 1, n), lax.rem(me + n - 1, n)
    edges = [
        remote(dec.at[1], halo.at[0], halo_send.at[0], halo_recv.at[0], patch=after),
        remote(dec.at[0], halo.at[1], halo_send.at[1], halo_recv.at[1], patch=prior),
    ]
    for copy in edges:
        copy.start()
    for copy in edges:
        copy.wait_recv()
    lines = [
        jnp.where(me > 0, halo[0].astype(F32), 0.0),
        dec[0].astype(F32),
        dec[1].astype(F32),
        jnp.where(me < n - 1, halo[1].astype(F32), 0.0),
    ]
    width = dec.shape[2]
    column = iota((LAT_CH, width), 1)
    shifted = []
    for line in lines:
        before_it = jnp.where(column == 0, 0.0, pltpu.roll(line, 1, 1))
        after_it = jnp.where(column == width - 1, 0.0, pltpu.roll(line, width - 1, 1))
        shifted.append([x.astype(BF16) for x in (before_it, line, after_it)])
    conv_col = to_column(conv_bias[...])
    for a in range(2):
        stencil = jnp.concatenate([shifted[a + u][v] for u in range(3) for v in range(3)], axis=0)
        result = lax.dot_general(conv_t[...], stencil, TN, preferred_element_type=F32)
        out[a] = (result + conv_col).astype(BF16)

    sent()
    for h in range(heads):
        published(h)
    peers(n, lambda d: rs_copy(d).wait_send())
    peers(nz, lambda d: z_copy(d).wait_send())
    peers(nz, lambda d: zg_copy(d).wait_send())
    peers(n, lambda d: ag_copy(d).wait_send())
    for copy in edges:
        copy.wait_send()


def on_device(
    n,
    nz,
    fresh_qkv,
    kv_cache,
    hidden,
    refresh,
    out_weight,
    final_weight,
    final_bias,
    gate_scale,
    noise_level,
    noisy_latent,
    velocity_cache,
    conv_weight,
    conv_bias,
):
    tok, _, local = fresh_qkv.shape
    heads = local // HEAD_DIM
    depth, vec = final_weight.shape
    rows = vec // n
    assert nz == REFRESH
    width = noisy_latent.shape[2]
    channels = conv_weight.shape[0]
    vmem, smem, anyw = (pl.BlockSpec(memory_space=m) for m in (pltpu.VMEM, pltpu.SMEM, pl.ANY))
    dma = pltpu.SemaphoreType.DMA
    kinds = 8 if n == 8 else n
    scratch = (
        [pltpu.VMEM((n, tok, HEAD_DIM), BF16)] * q_slots(n, heads)
        + [pltpu.VMEM((n, 2 * REFRESH, tok), F32)] * heads
        + [pltpu.VMEM((max(n // 2, 1), 2 * REFRESH, tok), F32)] * heads
        + [
            pltpu.VMEM((2, tok, local), BF16),
            pltpu.VMEM((tok, depth), BF16),
            pltpu.VMEM((local, depth), BF16),
            pltpu.VMEM((tok, local), BF16),
            pltpu.VMEM((heads, HEAD_DIM, tok), BF16),
            pltpu.VMEM((2 * vec, local), BF16),
            pltpu.VMEM((heads, REFRESH, vec, tok), F32),
            pltpu.VMEM((2 * tok, 2 * tok), BF16),
            pltpu.VMEM((vec, tok), F32),
            pltpu.VMEM((vec, depth), BF16),
            pltpu.VMEM((REFRESH, HEAD_DIM, tok), F32),
            pltpu.VMEM((n, REFRESH * rows, tok), BF16 if rows % 8 == 0 else F32),
            pltpu.VMEM((n, REFRESH * rows, tok), BF16 if rows % 8 == 0 else F32),
            pltpu.VMEM((nz, rows, tok), F32),
            pltpu.VMEM((nz, rows, tok), F32),
            pltpu.VMEM((nz, rows, tok), F32),
            pltpu.VMEM((n, rows, tok), F32),
            pltpu.VMEM((n, rows, tok), F32),
            pltpu.VMEM((2, LAT_CH, width), BF16),
            pltpu.VMEM((2, LAT_CH, width), BF16),
            dma((4,)),
            dma((heads,)),
            dma((heads, kinds)),
            dma((heads, kinds)),
            dma((heads, n)),
            dma((heads, n)),
            dma((n,)),
            dma((n,)),
            dma((nz,)),
            dma((nz,)),
            dma((nz,)),
            dma((nz,)),
            dma((n,)),
            dma((n,)),
            dma((2,)),
            dma((2,)),
            pltpu.SemaphoreType.REGULAR((heads,)),
        ]
    )
    return pl.pallas_call(
        functools.partial(kernel, n, nz, heads, tok),
        out_shape=jax.ShapeDtypeStruct((2, channels, width), BF16),
        in_specs=[smem, smem, anyw, vmem, anyw, anyw] + [vmem] * 7,
        out_specs=vmem,
        scratch_shapes=scratch,
        compiler_params=pltpu.CompilerParams(
            collective_id=0, has_side_effects=True, vmem_limit_bytes=58 * 1024 * 1024
        ),
    )(
        refresh,
        noise_level,
        jnp.transpose(fresh_qkv, (1, 0, 2)),
        kv_cache,
        hidden,
        out_weight,
        final_weight.T,
        final_bias[None, :],
        gate_scale[None, :],
        noisy_latent,
        velocity_cache,
        jnp.transpose(conv_weight, (1, 2, 3, 0)).reshape(-1, channels),
        conv_bias[None, :],
    )


def solution(mesh):
    return jax.shard_map(
        functools.partial(on_device, mesh.shape["patch"], mesh.shape["head"]),
        mesh=mesh,
        in_specs=(
            P("patch", None, "head"),
            P("patch", None, "head"),
            P("patch", None),
            P(),
            P("head", None),
            P(),
            P(),
            P(),
            P(),
            P("patch", None, None),
            P("patch", None, None),
            P("head", None, None, None),
            P("head"),
        ),
        out_specs=P("patch", "head", None),
        check_vma=False,
    )
```
